256 devices in a mesh: cond: 16 (over x_lo, y, core), slab: 16 (over x_hi, z).
Axes of the slice: x: 4 (x_hi: 2, x_lo: 2; x = x_hi * 2 + x_lo), y: 4, z: 8, core: 2. Of those that a mesh axis runs over, the one named last changes fastest.
Arguments:
- features: bfloat16 [16, 32, 16, 64, 128], P('cond', 'slab'), as said below
- latent: float32 [4, 32, 1024], P(None, 'slab', 'cond'), may hold values from -6 to 6
- cond_codes: int32 [16, 8], P('cond'), may hold values from 0 to 15
- guide_codes: int32 [16], replicated, may hold values from 1 to 8
- timestep: int32 [1], replicated, may hold values from 50 to 800
- code_table: float32 [8, 16, 256], replicated, may hold values from -2.5 to 2.5
- time_weight: float32 [256, 256], replicated, may hold values from -0.375 to 0.375
- film_weight: float32 [256, 256], replicated, may hold values from -0.375 to 0.375
- conv_one: bfloat16 [3, 3, 3, 128, 128], replicated, may hold values from -0.109375 to 0.109375
- conv_two: bfloat16 [3, 3, 3, 128, 128], replicated, may hold values from -0.109375 to 0.109375
- head_weight: float32 [128, 4], replicated, may hold values from -0.5 to 0.5
Outputs:
- guided: float32 [4, 32, 1024], P(None, 'slab', 'cond')
- stepped: float32 [4, 32, 1024], P(None, 'slab', 'cond')
The draws below stay inside these ranges and needn't reach their ends.
Inputs may be any that keep to these rules, and one draw needn't show every extreme that they name: `features`: finite values, up to about 60 in magnitude.
All inputs are finite; a program needn't handle non-finite values.
Results may differ from the reference program's by a relative error of at most 0.0026.
Values may be sent and summed in bfloat16 or wider, within the bound.
No kernel may reach another device: no remote copies, remote signals or barrier semaphores. Data moves between devices by JAX's collectives and lax.ppermute only.
A program may use at most 64 MiB of HBM per device.

```python
import math
import jax
import jax.numpy as jnp
from jax import lax

C = 128
GROUPS = 32
EMB = 256
LAT = 4
SLOTS = 8
CODES = 16
STRIDE = 20
H = 16
W = 64
TERMS = 16
DEPTH = 32
HW = 1024


def draw_features(key, part):
    key = jax.random.fold_in(key, 5)
    key_base = jax.random.fold_in(key, 0)
    key_chan = jax.random.fold_in(key, 1)
    key_layer = jax.random.fold_in(key, 3)
    key_mixed = jax.random.fold_in(key, 4)
    depth_index = jnp.arange(DEPTH, dtype=jnp.float32)
    rising = jnp.exp(math.log(3.0) * depth_index / max(DEPTH - 1, 1))
    chan_scale = jnp.exp(jax.random.uniform(key_chan, (C,), jnp.float32, 0.0, math.log(10.0))) / 3.0
    layer_scale = jnp.exp(jax.random.uniform(key_layer, (TERMS, DEPTH, 1, 1, 1), jnp.float32, -math.log(4.0), 0.0))
    mixed_scale = jnp.exp(jax.random.uniform(key_mixed, (TERMS, DEPTH, 1, 1, C), jnp.float32, -math.log(2.0), 0.0))
    base = jnp.clip(jax.random.normal(key_base, (TERMS, DEPTH, H, W, C), jnp.float32), -6.0, 6.0)
    values = base * rising[None, :, None, None, None] * chan_scale * layer_scale * mixed_scale
    return values.astype(jnp.bfloat16)


def set_ends(result, own_key, smallest, high):
    longest = result.shape.index(max(result.shape))
    spots = []
    for shift in (0, 1):
        where = [jax.random.randint(jax.random.fold_in(own_key, axis), (), 0, length) for axis, length in enumerate(result.shape)]
        where[longest] = (where[longest] + shift) % result.shape[longest]
        spots.append(tuple(where))
    return result.at[spots[0]].set(smallest).at[spots[1]].set(high)


def level_of(stream_key, extent, pieces, smallest, largest):
    gain, own = 1.0, jax.random.fold_in(stream_key, 6)
    for axis_at, shards_of in pieces:
        heights = jnp.exp(jax.random.uniform(jax.random.fold_in(own, axis_at), (shards_of,), jnp.float32, smallest / len(pieces), largest / len(pieces)))
        gain = gain * jnp.repeat(heights, extent[axis_at] // shards_of).reshape([-1 if axis == axis_at else 1 for axis in range(len(extent))])
    return gain


def normal_values(rng, extent, scale, reach, pieces=(), kind=jnp.bfloat16):
    values = scale * jax.random.normal(rng, extent, jnp.float32)
    if pieces:
        values = values * level_of(rng, extent, pieces, -0.22, 0.18)
    return jnp.clip(values, -reach, reach).astype(kind)


def setup_inputs(seed: int = 0) -> dict:
    keys = jax.random.split(jax.random.key(seed), 12)
    return {
        "features": draw_features(jax.random.fold_in(keys[11], 71), 0),
        "latent": normal_values(keys[1], (LAT, DEPTH, HW), 1.0, 6.0, ((1, 16), (2, 16)), jnp.float32),
        "cond_codes": set_ends(jax.random.randint(keys[2], (TERMS, SLOTS), 0, CODES), jax.random.fold_in(keys[2], 1), 0, CODES - 1).astype(jnp.int32),
        "guide_codes": set_ends(jax.random.randint(keys[3], (TERMS,), 1, 9), jax.random.fold_in(keys[3], 1), 1, 8).astype(jnp.int32),
        "timestep": jax.random.randint(keys[4], (1,), 50, 801).astype(jnp.int32),
        "code_table": normal_values(keys[5], (SLOTS, CODES, EMB), 0.35, 2.5, (), jnp.float32),
        "time_weight": normal_values(keys[6], (EMB, EMB), EMB ** -0.5, 0.375, (), jnp.float32),
        "film_weight": normal_values(keys[7], (EMB, 2 * C), EMB ** -0.5, 0.375, (), jnp.float32),
        "conv_one": normal_values(keys[8], (3, 3, 3, C, C), (27 * C) ** -0.5, 0.109375),
        "conv_two": normal_values(keys[9], (3, 3, 3, C, C), (27 * C) ** -0.5, 0.109375),
        "head_weight": normal_values(keys[10], (C, LAT), C ** -0.5, 0.5, (), jnp.float32),
    }


def embed_terms(code_row, time_value, code_table, time_weight, film_weight):
    one_hot = (code_row[:, None] == jnp.arange(CODES, dtype=jnp.int32)[None, :]).astype(jnp.float32)
    code_part = jnp.einsum('jc,jce->e', one_hot, code_table, precision=lax.Precision.HIGHEST)
    half_width = EMB // 2
    frequency = jnp.exp(-math.log(10000.0) * jnp.arange(half_width, dtype=jnp.float32) / half_width)
    angles = time_value * frequency
    sinus = jnp.concatenate([jnp.cos(angles), jnp.sin(angles)])
    embedding = jax.nn.silu(jnp.dot(sinus, time_weight, precision=lax.Precision.HIGHEST) + code_part)
    return jnp.dot(embedding, film_weight, precision=lax.Precision.HIGHEST)

def group_norm(values):
    per_group = C // GROUPS
    grouped = values.reshape(values.shape[:3] + (GROUPS, per_group))
    average = lax.optimization_barrier(jnp.mean(grouped, axis=(0, 1, 2, 4)))
    centred = grouped - average[:, None]
    spread = lax.optimization_barrier(jnp.mean(centred * centred, axis=(0, 1, 2, 4)))
    return (centred / jnp.sqrt(spread[:, None] + 1e-05)).reshape(values.shape)

def convolve(planes, weight):
    depth_out = planes.shape[0] - 2
    padded = jnp.pad(planes, ((0, 0), (1, 1), (1, 1), (0, 0)))
    summed = jnp.zeros((depth_out * H * W, C), jnp.float32)
    for depth_tap in range(3):
        for row_tap in range(3):
            columns = jnp.concatenate([padded[depth_tap:depth_tap + depth_out, row_tap:row_tap + H, col_tap:col_tap + W] for col_tap in range(3)], axis=-1)
            summed = summed + jnp.dot(columns.reshape(-1, 3 * C), weight[depth_tap, row_tap].reshape(3 * C, C), preferred_element_type=jnp.float32)
    return summed.reshape(depth_out, H, W, C)

def plan(step_value):
    frac = (step_value / 1000.0 + 0.008) / 1.008
    return jnp.cos(frac * math.pi / 2.0) ** 2

def reference(features, latent, cond_codes, guide_codes, timestep, code_table, time_weight, film_weight, conv_one, conv_two, head_weight):
    time_value = timestep[0].astype(jnp.float32)

    def one_term(pair):
        term_features, code_row = pair
        modulation = embed_terms(code_row, time_value, code_table, time_weight, film_weight)
        stretch = modulation[:C]
        offset = modulation[C:]
        base = term_features.astype(jnp.float32)
        first_act = jax.nn.silu(group_norm(base)).astype(jnp.bfloat16)
        first_conv = convolve(jnp.pad(first_act, ((1, 1), (0, 0), (0, 0), (0, 0))), conv_one)
        second_act = jax.nn.silu(group_norm(first_conv) * (1.0 + stretch) + offset).astype(jnp.bfloat16)
        second_conv = convolve(jnp.pad(second_act, ((1, 1), (0, 0), (0, 0), (0, 0))), conv_two)
        output = base + second_conv
        noise_pred = jnp.einsum('dhwc,cl->ldhw', output, head_weight, precision=lax.Precision.HIGHEST)
        return noise_pred.reshape(LAT, DEPTH, H * W)
    noise_all = lax.map(one_term, (features, cond_codes))
    term_weights = guide_codes.astype(jnp.float32) / 16.0
    others = jnp.sum(term_weights[1:])
    term_weights = term_weights.at[0].set(1.0 - others)
    guided = jnp.einsum('t,tldx->ldx', term_weights, noise_all, precision=lax.Precision.HIGHEST)
    now_bar = plan(time_value)
    next_bar = plan(time_value - STRIDE)
    clean = (latent - jnp.sqrt(1.0 - now_bar) * guided) / jnp.sqrt(now_bar)
    stepped = jnp.sqrt(next_bar) * clean + jnp.sqrt(1.0 - next_bar) * guided
    return (guided, stepped)
```

```python
import math

import jax
import jax.numpy as jnp
from jax import lax
from jax.sharding import PartitionSpec as P

C = 128
GROUPS = 32
EMB = 256
LAT = 4
CODES = 16
STRIDE = 20
DEP_DEV = 2
H = 16
W = 64


def with_halo(block, sides, width):
    for axis, dim in sides:
        count = lax.axis_size(axis)
        forward = [(i, i + 1) for i in range(count - 1)]
        backward = [(target, source) for source, target in forward]
        low = lax.ppermute(
            lax.slice_in_dim(block, block.shape[dim] - width, None, axis=dim), axis, forward
        )
        high = lax.ppermute(lax.slice_in_dim(block, 0, width, axis=dim), axis, backward)
        block = jnp.concatenate([low, block, high], axis=dim)
    return block


def embed_terms(code_row, time_value, code_table, time_weight, film_weight):
    one_hot = (code_row[:, None] == jnp.arange(CODES, dtype=jnp.int32)[None, :]).astype(jnp.float32)
    code_part = jnp.einsum("jc,jce->e", one_hot, code_table, precision=lax.Precision.HIGHEST)
    half_width = EMB // 2
    frequency = jnp.exp(-math.log(10000.0) * jnp.arange(half_width, dtype=jnp.float32) / half_width)
    angles = time_value * frequency
    sinus = jnp.concatenate([jnp.cos(angles), jnp.sin(angles)])
    embedding = jax.nn.silu(
        jnp.dot(sinus, time_weight, precision=lax.Precision.HIGHEST) + code_part
    )
    return jnp.dot(embedding, film_weight, precision=lax.Precision.HIGHEST)


def spread_out(values):
    return lax.all_to_all(
        jnp.broadcast_to(values[None], (lax.axis_size("slab"),) + values.shape), "slab", 0, 0
    )


def fold(values):
    return values.reshape(values.shape[:-1] + (GROUPS, C // GROUPS)).sum(axis=-1)


def group_stats(values, members):
    per_group = C // GROUPS
    cells = float(values.shape[0] * values.shape[1] * values.shape[2])
    own_sum = jnp.sum(values, axis=(0, 1, 2))
    centred = values - own_sum / cells
    own_square = jnp.sum(centred * centred, axis=(0, 1, 2))
    every = spread_out(jnp.stack([own_sum, own_square]))
    average = fold(every[:, 0].sum(axis=0)) / members
    apart = every[:, 0] / cells - jnp.repeat(average, per_group)
    spread = fold((every[:, 1] + cells * apart * apart).sum(axis=0)) / members
    return (average, spread)


def normalize(values, average, spread):
    per_group = C // GROUPS
    return (values - jnp.repeat(average, per_group)) / jnp.sqrt(
        jnp.repeat(spread, per_group) + 1e-05
    )


def convolve(planes, weight):
    depth_out = planes.shape[0] - 2
    padded = jnp.pad(planes, ((0, 0), (1, 1), (1, 1), (0, 0)))
    summed = jnp.zeros((depth_out * H * W, C), jnp.float32)
    for depth_tap in range(3):
        for row_tap in range(3):
            columns = jnp.concatenate(
                [
                    padded[
                        depth_tap : depth_tap + depth_out,
                        row_tap : row_tap + H,
                        col_tap : col_tap + W,
                    ]
                    for col_tap in range(3)
                ],
                axis=-1,
            )
            summed = summed + jnp.dot(
                columns.reshape(-1, 3 * C),
                weight[depth_tap, row_tap].reshape(3 * C, C),
                preferred_element_type=jnp.float32,
            )
    return summed.reshape(depth_out, H, W, C)


def plane_rims(values):
    return with_halo(values, (("slab", 0),), 1)


def plan(step_value):
    frac = (step_value / 1000.0 + 0.008) / 1.008
    return jnp.cos(frac * math.pi / 2.0) ** 2


def per_device(
    features,
    latent,
    cond_codes,
    guide_codes,
    timestep,
    code_table,
    time_weight,
    film_weight,
    conv_one,
    conv_two,
    head_weight,
):
    slab_count = lax.axis_size("slab")
    depth_all = DEP_DEV * slab_count
    members = float(depth_all * H * W * (C // GROUPS))
    time_value = timestep[0].astype(jnp.float32)
    modulation = embed_terms(cond_codes[0], time_value, code_table, time_weight, film_weight)
    stretch = modulation[:C]
    offset = modulation[C:]
    base = features[0].astype(jnp.float32)
    average, spread = group_stats(base, members)
    rims = plane_rims(features[0])
    slab_index = lax.axis_index("slab")
    depth_at = slab_index * DEP_DEV - 1 + jnp.arange(DEP_DEV + 2)
    inside = ((depth_at >= 0) & (depth_at < depth_all))[:, None, None, None]
    first_act = jax.nn.silu(normalize(rims.astype(jnp.float32), average, spread))
    first_act = jnp.where(inside, first_act, 0.0).astype(jnp.bfloat16)
    first_conv = convolve(first_act, conv_one)
    average_two, spread_two = group_stats(first_conv, members)
    second_act = jax.nn.silu(
        normalize(first_conv, average_two, spread_two) * (1.0 + stretch) + offset
    ).astype(jnp.bfloat16)
    second_conv = convolve(plane_rims(second_act), conv_two)
    output = base + second_conv
    noise_pred = jnp.einsum(
        "dhwc,cl->ldhw", output, head_weight, precision=lax.Precision.HIGHEST
    ).reshape(LAT, DEP_DEV, H * W)
    term_count = lax.axis_size("cond")
    term_index = lax.axis_index("cond")
    term_weights = guide_codes.astype(jnp.float32) / 16.0
    others = jnp.sum(term_weights[1:])
    term_weights = term_weights.at[0].set(1.0 - others)
    own_weight = jnp.sum(
        jnp.where(jnp.arange(term_count, dtype=jnp.int32) == term_index, term_weights, 0.0)
    )
    weighted = own_weight * noise_pred
    share_width = H * W // term_count
    pieces = weighted.reshape(LAT, DEP_DEV, term_count, share_width).transpose(2, 0, 1, 3)
    guided = lax.all_to_all(pieces, "cond", 0, 0).sum(axis=0)
    now_bar = plan(time_value)
    next_bar = plan(time_value - STRIDE)
    clean = (latent - jnp.sqrt(1.0 - now_bar) * guided) / jnp.sqrt(now_bar)
    stepped = jnp.sqrt(next_bar) * clean + jnp.sqrt(1.0 - next_bar) * guided
    return (guided, stepped)


def solution(mesh):
    placed = (
        P("cond", "slab", None, None, None),
        P(None, "slab", "cond"),
        P("cond", None),
        P(),
        P(),
        P(),
        P(),
        P(),
        P(),
        P(),
        P(),
    )
    return jax.shard_map(
        per_device,
        mesh=mesh,
        in_specs=placed,
        out_specs=(P(None, "slab", "cond"), P(None, "slab", "cond")),
        check_vma=False,
    )
```

```python
import math

import jax
import jax.numpy as jnp
from jax import lax
from jax.experimental import pallas as pl
from jax.experimental.pallas import tpu as pltpu
from jax.sharding import PartitionSpec as P

C = 128
GROUPS = 32
PER_GROUP = C // GROUPS
EMB = 256
LAT = 4
SLOTS = 8
STRIDE = 20
DEP_DEV = 2
H = 16
W = 64
HW = H * W
TERMS = 16
SHARE = HW // TERMS
SLABS = 16
CELLS = DEP_DEV * HW
MEMBERS = float(SLABS * CELLS * PER_GROUP)
TAPS = 27
F32 = jnp.float32
BF16 = jnp.bfloat16
ROWS = 2 * LAT

VMEM = pl.BlockSpec(memory_space=pltpu.VMEM)
SMEM = pl.BlockSpec(memory_space=pltpu.SMEM)
ANY = pl.BlockSpec(memory_space=pl.ANY)
PARAMS = pltpu.CompilerParams(vmem_limit_bytes=32 * 1024 * 1024)


def dot_last(left, right):
    return lax.dot_general(left, right, (((1,), (1,)), ((), ())), preferred_element_type=F32)


def silu(values):
    half = 0.5 * values
    return half + half * jnp.tanh(half)


def own_stats(values, out_ref):
    total = jnp.sum(values, axis=0, keepdims=True)
    centred = values - total * (1.0 / CELLS)
    square = jnp.sum(centred * centred, axis=0, keepdims=True)
    both = jnp.concatenate([total, square], axis=0)
    out_ref[...] = jnp.broadcast_to(both[None], (SLABS, 2, C))


def group_matrix():
    row = lax.broadcasted_iota(jnp.int32, (C, C), 0) // PER_GROUP
    column = lax.broadcasted_iota(jnp.int32, (C, C), 1) // PER_GROUP
    return (row == column).astype(F32)


def over_group(values, matrix):
    wide = jnp.broadcast_to(values, (8, C))
    return jnp.dot(wide, matrix, precision=lax.Precision.HIGHEST, preferred_element_type=F32)[:1]


def all_stats(every_ref):
    every = every_ref[...]
    totals = every[:, 0, :]
    squares = every[:, 1, :]
    matrix = group_matrix()
    average = over_group(jnp.sum(totals, axis=0, keepdims=True), matrix) / MEMBERS
    apart = totals * (1.0 / CELLS) - average
    spread = (
        over_group(jnp.sum(squares + CELLS * (apart * apart), axis=0, keepdims=True), matrix)
        / MEMBERS
    )
    return average, 1.0 / jnp.sqrt(spread + 1e-05)


def stats_kernel(features, out, low, high, held, sems):
    load = pltpu.make_async_copy(features, held, sems.at[0])
    first = pltpu.make_async_copy(features.at[0], low, sems.at[1])
    last = pltpu.make_async_copy(features.at[DEP_DEV - 1], high, sems.at[2])
    load.start()
    first.start()
    last.start()
    load.wait()
    own_stats(held[...].reshape(CELLS, C).astype(F32), out)
    first.wait()
    last.wait()


def stats_call(features):
    plane = jax.ShapeDtypeStruct((HW, C), BF16)
    return pl.pallas_call(
        stats_kernel,
        out_shape=(jax.ShapeDtypeStruct((SLABS, 2, C), F32), plane, plane),
        in_specs=[ANY],
        out_specs=(VMEM, ANY, ANY),
        scratch_shapes=[pltpu.VMEM((DEP_DEV, HW, C), BF16), pltpu.SemaphoreType.DMA((3,))],
        compiler_params=PARAMS,
        name="stats",
    )(features)


def three_parts(values):
    high = values.astype(BF16).astype(F32)
    rest = values - high
    middle = rest.astype(BF16).astype(F32)
    low = rest - middle
    zero = jnp.zeros_like(values)
    return jnp.concatenate([high, middle, low, zero], axis=0).astype(BF16)


def prep_kernel(
    codes, guides, term, sinus, table, time_weight, film, conv_two, head, features, mod, base, mix
):
    def exact(left, right):
        return jnp.dot(left, right, precision=lax.Precision.HIGHEST, preferred_element_type=F32)

    embedding = exact(jnp.broadcast_to(sinus[...], (8, EMB)), time_weight[...])[:1]
    code_part = jnp.zeros((1, EMB), F32)
    for slot in range(SLOTS):
        code_part = code_part + table[slot, pl.ds(codes[0, slot], 1), :]
    embedding = silu(embedding + code_part)
    mod[...] = exact(jnp.broadcast_to(embedding, (8, EMB)), film[...])

    others = guides[1]
    for at in range(2, TERMS):
        others = others + guides[at]
    own = jnp.where(term[0] == 0, TERMS - others, guides[term[0]])
    weight = own.astype(F32) * (1.0 / 16.0)

    head_rows = jnp.concatenate([head[...], head[...]], axis=0)
    upper = lax.broadcasted_iota(jnp.int32, (ROWS, C), 0) < LAT
    parts = three_parts(head_rows)
    composed = dot_last(parts, conv_two[...])
    composed = (
        composed[:ROWS] + (composed[ROWS : 2 * ROWS] + composed[2 * ROWS : 3 * ROWS])
    ) * weight
    nothing = jnp.zeros((ROWS, C), F32)
    for near in range(9):
        for plane in range(DEP_DEV + 2):
            at = [
                composed[:, (tap * 9 + near) * C : (tap * 9 + near + 1) * C]
                if 0 <= tap < 3
                else nothing
                for tap in (plane, plane - 1)
            ]
            mix[near * ROWS : (near + 1) * ROWS, plane * C : (plane + 1) * C] = jnp.where(
                upper, at[0], at[1]
            )

    wide = jnp.concatenate(
        [jnp.where(upper, head_rows, 0.0), jnp.where(upper, 0.0, head_rows)], axis=1
    )
    both = jnp.concatenate([features[0], features[1]], axis=1)
    direct = dot_last(three_parts(wide), both)
    base[...] = (direct[:ROWS] + (direct[ROWS : 2 * ROWS] + direct[2 * ROWS : 3 * ROWS])) * weight


def prep_call(codes, guides, term, sinus, table, time_weight, film, conv_two, head, features):
    return pl.pallas_call(
        prep_kernel,
        out_shape=(
            jax.ShapeDtypeStruct((8, 2 * C), F32),
            jax.ShapeDtypeStruct((ROWS, HW), F32),
            jax.ShapeDtypeStruct((9 * ROWS, 4 * C), F32),
        ),
        in_specs=[SMEM, SMEM, SMEM] + [VMEM] * 7,
        out_specs=(VMEM, VMEM, VMEM),
        compiler_params=PARAMS,
        cost_estimate=pl.CostEstimate(
            flops=200_000_000, bytes_accessed=3_000_000, transcendentals=512
        ),
        name="prep",
    )(codes, guides, term, sinus, table, time_weight, film, conv_two, head, features)


def conv_kernel(edges, every, low, own, high, weight, out, out_low, out_high, out_stats, held, side):
    average, scale = all_stats(every)
    shift = -average * scale
    held[0:W, :] = jnp.zeros((W, 4 * C), BF16)
    held[W + HW :, :] = jnp.zeros((W, 4 * C), BF16)
    for plane, (source, edge) in enumerate(
        [(low, 0), (own.at[0], None), (own.at[1], None), (high, 1)]
    ):
        values = silu(source[...].astype(F32) * scale + shift)
        if edge is not None:
            values = values * edges[edge]
        held[W : W + HW, plane * C : (plane + 1) * C] = values.astype(BF16)

    zero = jnp.zeros((C, C), BF16)
    column = lax.broadcasted_iota(jnp.int32, (HW, C), 0) % W

    def taps(col):
        blocks = []
        for row in range(3):
            for plane in range(4):
                pair = [
                    weight[((tap * 3 + row) * 3 + col) * C : ((tap * 3 + row) * 3 + col + 1) * C, :]
                    if 0 <= tap < 3
                    else zero
                    for tap in (plane, plane - 1)
                ]
                blocks.append(jnp.concatenate(pair, axis=1))
        return jnp.concatenate(blocks, axis=0)

    left = jnp.concatenate([held[row * W : row * W + HW, :] for row in range(3)], axis=1)
    products = [
        jnp.dot(left, taps(col), preferred_element_type=F32) for col in range(3)
    ]
    planes = []
    for plane in range(DEP_DEV):
        part = [product[:, plane * C : (plane + 1) * C] for product in products]
        side[8 : 8 + HW, :] = part[0]
        before = jnp.where(column == 0, 0.0, side[7 : 7 + HW, :])
        side[8 : 8 + HW, :] = part[2]
        after = jnp.where(column == W - 1, 0.0, side[9 : 9 + HW, :])
        values = part[1] + before + after
        out[plane] = values
        planes.append(values)
    out_low[...] = planes[0].astype(BF16)
    out_high[...] = planes[1].astype(BF16)
    own_stats(jnp.concatenate(planes, axis=0), out_stats)


def conv_call(edges, every, low, own, high, weight):
    plane = jax.ShapeDtypeStruct((HW, C), BF16)
    return pl.pallas_call(
        conv_kernel,
        out_shape=(
            jax.ShapeDtypeStruct((DEP_DEV, HW, C), F32),
            plane,
            plane,
            jax.ShapeDtypeStruct((SLABS, 2, C), F32),
        ),
        in_specs=[SMEM] + [VMEM] * 5,
        out_specs=(VMEM,) * 4,
        scratch_shapes=[
            pltpu.VMEM((HW + 2 * W, 4 * C), BF16),
            pltpu.VMEM((HW + 16, C), F32),
        ],
        compiler_params=PARAMS,
        cost_estimate=pl.CostEstimate(
            flops=2_500_000_000, bytes_accessed=4_000_000, transcendentals=500_000
        ),
        name="conv",
    )(edges, every, low, own, high, weight)


def head_kernel(edges, every, low, own, high, mod, base, mix, out, held):
    average, scale = all_stats(every)
    factor = scale * (1.0 + mod[0:1, :C])
    shift = mod[0:1, C:] - average * factor
    for plane, (source, edge) in enumerate(
        [(low, 0), (own.at[0], None), (own.at[1], None), (high, 1)]
    ):
        values = silu(source[...].astype(F32) * factor + shift)
        if edge is not None:
            values = values * edges[edge]
        held[:, plane * C : (plane + 1) * C] = values.astype(BF16)
    weights = mix[...]
    coarse = weights.astype(BF16).astype(F32)
    pair = jnp.concatenate([coarse, weights - coarse], axis=0).astype(BF16)
    product = dot_last(pair, held[...])
    product = product[: 9 * ROWS] + product[9 * ROWS :]
    at = lax.broadcasted_iota(jnp.int32, (ROWS, HW), 1)
    summed = base[...]
    for col in range(3):
        part = [product[(row * 3 + col) * ROWS : (row * 3 + col + 1) * ROWS] for row in range(3)]
        values = (
            part[1]
            + jnp.where(at < W, 0.0, pltpu.roll(part[0], W, 1))
            + jnp.where(at >= HW - W, 0.0, pltpu.roll(part[2], HW - W, 1))
        )
        if col == 0:
            values = jnp.where(at % W == 0, 0.0, pltpu.roll(values, 1, 1))
        if col == 2:
            values = jnp.where(at % W == W - 1, 0.0, pltpu.roll(values, HW - 1, 1))
        summed = summed + values
    for target in range(TERMS):
        piece = summed[:, target * SHARE : (target + 1) * SHARE]
        out[target] = jnp.concatenate([piece[:LAT], piece[LAT:]], axis=1)


def head_call(edges, every, low, own, high, mod, base, mix):
    return pl.pallas_call(
        head_kernel,
        out_shape=jax.ShapeDtypeStruct((TERMS, LAT, DEP_DEV * SHARE), F32),
        in_specs=[SMEM] + [VMEM] * 7,
        out_specs=VMEM,
        scratch_shapes=[pltpu.VMEM((HW, 4 * C), BF16)],
        compiler_params=PARAMS,
        name="head",
    )(edges, every, low, own, high, mod, base, mix)


def final_kernel(roots, pieces, latent, guided, stepped):
    total = jnp.sum(pieces[...], axis=0)
    for plane in range(DEP_DEV):
        value = total[:, plane * SHARE : (plane + 1) * SHARE]
        clean = (latent[:, plane, :] - roots[0] * value) / roots[1]
        guided[:, plane, :] = value
        stepped[:, plane, :] = roots[2] * clean + roots[3] * value


def final_call(roots, pieces, latent):
    shape = jax.ShapeDtypeStruct((LAT, DEP_DEV, SHARE), F32)
    return pl.pallas_call(
        final_kernel,
        out_shape=(shape, shape),
        in_specs=[SMEM, VMEM, VMEM],
        out_specs=(VMEM, VMEM),
        compiler_params=PARAMS,
        name="final",
    )(roots, pieces, latent)


def plan(step_value):
    frac = (step_value / 1000.0 + 0.008) / 1.008
    return jnp.cos(frac * math.pi / 2.0) ** 2


def rims(low, high):
    forward = [(i, i + 1) for i in range(SLABS - 1)]
    backward = [(i + 1, i) for i in range(SLABS - 1)]
    return lax.ppermute(high, "slab", forward), lax.ppermute(low, "slab", backward)


def per_device(
    features,
    latent,
    cond_codes,
    guide_codes,
    timestep,
    code_table,
    time_weight,
    film_weight,
    conv_one,
    conv_two,
    head_weight,
):
    planes = features.reshape(DEP_DEV, HW, C)
    slab_index = lax.axis_index("slab")
    edges = jnp.stack([slab_index > 0, slab_index < SLABS - 1]).astype(F32)
    term = lax.axis_index("cond").astype(jnp.int32).reshape(1)
    time_value = timestep[0].astype(F32)
    half_width = EMB // 2
    frequency = jnp.exp(-math.log(10000.0) * jnp.arange(half_width, dtype=F32) / half_width)
    angles = time_value * frequency
    sinus = jnp.concatenate([jnp.cos(angles), jnp.sin(angles)]).reshape(1, EMB)
    now_bar = plan(time_value)
    next_bar = plan(time_value - STRIDE)
    roots = jnp.sqrt(jnp.stack([1.0 - now_bar, now_bar, next_bar, 1.0 - next_bar]))

    stats, low, high = stats_call(planes)
    below, above = rims(low, high)
    every = lax.all_to_all(stats, "slab", 0, 0)
    mod, base, mix = prep_call(
        cond_codes,
        guide_codes,
        term,
        sinus,
        code_table,
        time_weight,
        film_weight,
        conv_two.reshape(TAPS * C, C),
        head_weight.T,
        planes,
    )
    first, low, high, stats = conv_call(
        edges, every, below, planes, above, conv_one.reshape(TAPS * C, C)
    )
    below, above = rims(low, high)
    every = lax.all_to_all(stats, "slab", 0, 0)
    pieces = head_call(edges, every, below, first, above, mod, base, mix)
    pieces = lax.all_to_all(pieces, "cond", 0, 0)
    return final_call(roots, pieces, latent)


def solution(mesh):
    placed = (
        P("cond", "slab", None, None, None),
        P(None, "slab", "cond"),
        P("cond", None),
        P(),
        P(),
        P(),
        P(),
        P(),
        P(),
        P(),
        P(),
    )
    return jax.shard_map(
        per_device,
        mesh=mesh,
        in_specs=placed,
        out_specs=(P(None, "slab", "cond"), P(None, "slab", "cond")),
        check_vma=False,
    )
```

```python
import math

import jax
import jax.numpy as jnp
from jax import lax
from jax.experimental import pallas as pl
from jax.experimental.pallas import tpu as pltpu
from jax.sharding import PartitionSpec as P

C = 128
GROUPS = 32
PER_GROUP = C // GROUPS
EMB = 256
LAT = 4
SLOTS = 8
STRIDE = 20
DEP_DEV = 2
H = 16
W = 64
HW = H * W
TERMS = 16
SHARE = HW // TERMS
SLABS = 16
CELLS = DEP_DEV * HW
MEMBERS = float(SLABS * CELLS * PER_GROUP)
TAPS = 27
F32 = jnp.float32
BF16 = jnp.bfloat16
ROWS = 2 * LAT

VMEM = pl.BlockSpec(memory_space=pltpu.VMEM)
SMEM = pl.BlockSpec(memory_space=pltpu.SMEM)
ANY = pl.BlockSpec(memory_space=pl.ANY)
HBM = pl.BlockSpec(memory_space=pltpu.HBM)


def params(mebibytes):
    return pltpu.CompilerParams(vmem_limit_bytes=mebibytes * 1024 * 1024)


def dot_last(left, right):
    return lax.dot_general(left, right, (((1,), (1,)), ((), ())), preferred_element_type=F32)


def silu(values):
    half = 0.5 * values
    return half + half * jnp.tanh(half)


def own_stats(values, out_ref):
    total = jnp.sum(values, axis=0, keepdims=True)
    centred = values - total * (1.0 / CELLS)
    square = jnp.sum(centred * centred, axis=0, keepdims=True)
    both = jnp.concatenate([total, square], axis=0)
    out_ref[...] = jnp.broadcast_to(both[None], (SLABS, 2, C))


def group_matrix():
    row = lax.broadcasted_iota(jnp.int32, (C, C), 0) // PER_GROUP
    column = lax.broadcasted_iota(jnp.int32, (C, C), 1) // PER_GROUP
    return (row == column).astype(BF16)


def three_parts(values):
    high = values.astype(BF16).astype(F32)
    rest = values - high
    middle = rest.astype(BF16).astype(F32)
    low = rest - middle
    zero = jnp.zeros_like(values)
    return jnp.concatenate([high, middle, low, zero], axis=0).astype(BF16)


def over_group(values, matrix):
    wide = three_parts(jnp.broadcast_to(values, (8, C)))
    folded = jnp.dot(wide, matrix, preferred_element_type=F32)
    return folded[:1] + (folded[8:9] + folded[16:17])


def all_stats(every_ref):
    every = every_ref[...]
    totals = every[:, 0, :]
    squares = every[:, 1, :]
    matrix = group_matrix()
    average = over_group(jnp.sum(totals, axis=0, keepdims=True), matrix) / MEMBERS
    apart = totals * (1.0 / CELLS) - average
    spread = (
        over_group(jnp.sum(squares + CELLS * (apart * apart), axis=0, keepdims=True), matrix)
        / MEMBERS
    )
    return average, 1.0 / jnp.sqrt(spread + 1e-05)


def stats_kernel(features, out):
    own_stats(features[...].reshape(CELLS, C).astype(F32), out)


def stats_call(features):
    return pl.pallas_call(
        stats_kernel,
        out_shape=jax.ShapeDtypeStruct((SLABS, 2, C), F32),
        in_specs=[VMEM],
        out_specs=VMEM,
        compiler_params=params(4),
        name="stats",
    )(features)


def rims_kernel(planes, odd, even):
    parity = lax.axis_index("slab") % 2
    odd[...] = planes[parity]
    even[...] = planes[DEP_DEV - 1 - parity]


def rims_call(planes):
    plane = jax.ShapeDtypeStruct((HW, C), BF16)
    return pl.pallas_call(
        rims_kernel,
        out_shape=(plane, plane),
        in_specs=[VMEM],
        out_specs=(VMEM, VMEM),
        compiler_params=params(4),
        name="rims",
    )(planes)


def prep_kernel(
    codes,
    guides,
    sinus,
    roots,
    table,
    time_weight,
    film,
    conv_two,
    head,
    features,
    mod,
    base,
    mix,
    held_roots,
):
    held_roots[...] = jnp.broadcast_to(roots[...], (8, C))

    def exact(left, right):
        return jnp.dot(left, right, precision=lax.Precision.HIGHEST, preferred_element_type=F32)

    embedding = exact(jnp.broadcast_to(sinus[...], (8, EMB)), time_weight[...])[:1]
    code_part = jnp.zeros((1, EMB), F32)
    for slot in range(SLOTS):
        code_part = code_part + table[slot, pl.ds(codes[0, slot], 1), :]
    embedding = silu(embedding + code_part)
    mod[...] = exact(jnp.broadcast_to(embedding, (8, EMB)), film[...])

    others = guides[1]
    for at in range(2, TERMS):
        others = others + guides[at]
    term = lax.axis_index("cond")
    own = jnp.where(term == 0, TERMS - others, guides[term])
    weight = own.astype(F32) * (1.0 / 16.0)

    head_rows = jnp.concatenate([head[...], head[...]], axis=0)
    upper = lax.broadcasted_iota(jnp.int32, (ROWS, C), 0) < LAT
    parts = three_parts(head_rows)
    composed = dot_last(parts, conv_two[...])
    composed = (
        composed[:ROWS] + (composed[ROWS : 2 * ROWS] + composed[2 * ROWS : 3 * ROWS])
    ) * weight
    nothing = jnp.zeros((ROWS, C), F32)
    for near in range(9):
        for plane in range(DEP_DEV + 2):
            at = [
                composed[:, (tap * 9 + near) * C : (tap * 9 + near + 1) * C]
                if 0 <= tap < 3
                else nothing
                for tap in (plane, plane - 1)
            ]
            mix[near * ROWS : (near + 1) * ROWS, plane * C : (plane + 1) * C] = jnp.where(
                upper, at[0], at[1]
            )

    wide = jnp.concatenate(
        [jnp.where(upper, head_rows, 0.0), jnp.where(upper, 0.0, head_rows)], axis=1
    )
    both = jnp.concatenate([features[0], features[1]], axis=1)
    direct = dot_last(three_parts(wide), both)
    base[...] = (direct[:ROWS] + (direct[ROWS : 2 * ROWS] + direct[2 * ROWS : 3 * ROWS])) * weight


def prep_call(codes, guides, sinus, roots, table, time_weight, film, conv_two, head, features):
    return pl.pallas_call(
        prep_kernel,
        out_shape=(
            jax.ShapeDtypeStruct((8, 2 * C), F32),
            jax.ShapeDtypeStruct((ROWS, HW), F32),
            jax.ShapeDtypeStruct((9 * ROWS, 4 * C), F32),
            jax.ShapeDtypeStruct((8, C), F32),
        ),
        in_specs=[SMEM, SMEM] + [VMEM] * 8,
        out_specs=(VMEM,) * 4,
        compiler_params=params(8),
        cost_estimate=pl.CostEstimate(
            flops=200_000_000, bytes_accessed=3_000_000, transcendentals=512
        ),
        name="prep",
    )(codes, guides, sinus, roots, table, time_weight, film, conv_two, head, features)


def conv_part(planes, taps_of, weight, held, side):
    held[0:W, :] = jnp.zeros((W, 2 * C), BF16)
    held[W + HW :, :] = jnp.zeros((W, 2 * C), BF16)
    for at, values in enumerate(planes):
        held[W : W + HW, at * C : (at + 1) * C] = values.astype(BF16)
    zero = jnp.zeros((C, C), BF16)
    left = jnp.concatenate([held[row * W : row * W + HW, :] for row in range(3)], axis=1)

    def block(tap, row, col):
        at = ((tap * 3 + row) * 3 + col) * C
        return weight[at : at + C, :]

    products = []
    for col in range(3):
        right = jnp.concatenate(
            [
                jnp.concatenate(
                    [zero if tap is None else block(tap, row, col) for tap in taps], axis=1
                )
                for row in range(3)
                for taps in taps_of
            ],
            axis=0,
        )
        products.append(jnp.dot(left, right, preferred_element_type=F32))
    column = lax.broadcasted_iota(jnp.int32, (HW, C), 0) % W
    sums = []
    for plane in range(DEP_DEV):
        part = [product[:, plane * C : (plane + 1) * C] for product in products]
        side[8 : 8 + HW, :] = part[0]
        before = jnp.where(column == 0, 0.0, side[7 : 7 + HW, :])
        side[8 : 8 + HW, :] = part[2]
        after = jnp.where(column == W - 1, 0.0, side[9 : 9 + HW, :])
        sums.append(part[1] + before + after)
    return sums


def conv_scratch():
    return [pltpu.VMEM((HW + 2 * W, 2 * C), BF16), pltpu.VMEM((HW + 16, C), F32)]


def inner_kernel(every, own, weight, odd, out, norm, held, side):
    del odd
    average, scale = all_stats(every)
    shift = -average * scale
    norm[0:1, :] = scale
    norm[1:2, :] = shift
    planes = [silu(own[at].astype(F32) * scale + shift) for at in range(DEP_DEV)]
    sums = conv_part(planes, [(1, 0), (2, 1)], weight, held, side)
    for at in range(DEP_DEV):
        out[at] = sums[at]


def inner_call(every, own, weight, odd):
    return pl.pallas_call(
        inner_kernel,
        out_shape=(
            jax.ShapeDtypeStruct((DEP_DEV, HW, C), F32),
            jax.ShapeDtypeStruct((8, C), F32),
        ),
        in_specs=[VMEM] * 4,
        out_specs=(VMEM, VMEM),
        scratch_shapes=conv_scratch(),
        compiler_params=params(12),
        cost_estimate=pl.CostEstimate(
            flops=2_500_000_000, bytes_accessed=4_000_000, transcendentals=500_000
        ),
        name="inner",
    )(every, own, weight, odd)


def rim_planes(swapped):
    slab = lax.axis_index("slab")
    first = slab % 2 == 0
    low = jnp.where(first, swapped[1], swapped[0])
    high = jnp.where(first, swapped[0], swapped[1])
    return [jnp.where(slab > 0, low, 0.0), jnp.where(slab < SLABS - 1, high, 0.0)]


def outer_kernel(norm, odd, even, inner, weight, out, out_stats, out_odd, out_even, held, side):
    scale = norm[0:1, :]
    shift = norm[1:2, :]
    planes = rim_planes([silu(source[...].astype(F32) * scale + shift) for source in (even, odd)])
    sums = conv_part(planes, [(0, None), (None, 2)], weight, held, side)
    for at in range(DEP_DEV):
        out[at] = inner[at] + sums[at]
    own_stats(out[...].reshape(CELLS, C), out_stats)
    parity = lax.axis_index("slab") % 2
    out_odd[...] = out[parity].astype(BF16)
    out_even[...] = out[DEP_DEV - 1 - parity].astype(BF16)


def outer_call(norm, odd, even, inner, weight):
    return pl.pallas_call(
        outer_kernel,
        out_shape=(
            jax.ShapeDtypeStruct((DEP_DEV, HW, C), F32),
            jax.ShapeDtypeStruct((SLABS, 2, C), F32),
            jax.ShapeDtypeStruct((HW, C), BF16),
            jax.ShapeDtypeStruct((HW, C), BF16),
        ),
        in_specs=[VMEM] * 5,
        out_specs=(VMEM,) * 4,
        scratch_shapes=conv_scratch(),
        compiler_params=params(12),
        cost_estimate=pl.CostEstimate(
            flops=2_500_000_000, bytes_accessed=4_000_000, transcendentals=500_000
        ),
        name="outer",
    )(norm, odd, even, inner, weight)


def mixed(planes, weights, held):
    for at, values in enumerate(planes):
        held[:, at * C : (at + 1) * C] = values.astype(BF16)
    coarse = weights.astype(BF16).astype(F32)
    pair = jnp.concatenate([coarse, weights - coarse], axis=0).astype(BF16)
    product = dot_last(pair, held[...])
    return product[: 9 * ROWS] + product[9 * ROWS :]


def near_kernel(every, own, mod, mix, odd, out, norm, held):
    del odd
    average, scale = all_stats(every)
    factor = scale * (1.0 + mod[0:1, :C])
    shift = mod[0:1, C:] - average * factor
    norm[0:1, :] = factor
    norm[1:2, :] = shift
    planes = [silu(own[at] * factor + shift) for at in range(DEP_DEV)]
    out[...] = mixed(planes, mix[:, C : 3 * C], held)


def near_call(every, own, mod, mix, odd):
    return pl.pallas_call(
        near_kernel,
        out_shape=(
            jax.ShapeDtypeStruct((9 * ROWS, HW), F32),
            jax.ShapeDtypeStruct((8, C), F32),
        ),
        in_specs=[VMEM] * 5,
        out_specs=(VMEM, VMEM),
        scratch_shapes=[pltpu.VMEM((HW, 2 * C), BF16)],
        compiler_params=params(6),
        cost_estimate=pl.CostEstimate(
            flops=2_500_000_000, bytes_accessed=4_000_000, transcendentals=500_000
        ),
        name="near",
    )(every, own, mod, mix, odd)


def head_kernel(norm, odd, even, near, base, mix, out, held):
    factor = norm[0:1, :]
    shift = norm[1:2, :]
    planes = rim_planes([silu(source[...].astype(F32) * factor + shift) for source in (even, odd)])
    weights = jnp.concatenate([mix[:, :C], mix[:, 3 * C :]], axis=1)
    product = near[...] + mixed(planes, weights, held)
    at = lax.broadcasted_iota(jnp.int32, (ROWS, HW), 1)
    summed = base[...]
    for col in range(3):
        part = [product[(row * 3 + col) * ROWS : (row * 3 + col + 1) * ROWS] for row in range(3)]
        values = (
            part[1]
            + jnp.where(at < W, 0.0, pltpu.roll(part[0], W, 1))
            + jnp.where(at >= HW - W, 0.0, pltpu.roll(part[2], HW - W, 1))
        )
        if col == 0:
            values = jnp.where(at % W == 0, 0.0, pltpu.roll(values, 1, 1))
        if col == 2:
            values = jnp.where(at % W == W - 1, 0.0, pltpu.roll(values, HW - 1, 1))
        summed = summed + values
    for target in range(TERMS):
        piece = summed[:, target * SHARE : (target + 1) * SHARE]
        out[target] = jnp.concatenate([piece[:LAT], piece[LAT:]], axis=1)


def head_call(norm, odd, even, near, base, mix):
    return pl.pallas_call(
        head_kernel,
        out_shape=jax.ShapeDtypeStruct((TERMS, LAT, DEP_DEV * SHARE), F32),
        in_specs=[VMEM] * 6,
        out_specs=VMEM,
        scratch_shapes=[pltpu.VMEM((HW, 2 * C), BF16)],
        compiler_params=params(6),
        name="head",
    )(norm, odd, even, near, base, mix)


def final_kernel(roots, pieces, latent, guided, stepped):
    total = jnp.sum(pieces[...], axis=0)
    noise_now, root_now, root_next, noise_next = [roots[0, at * 32] for at in range(4)]
    for plane in range(DEP_DEV):
        value = total[:, plane * SHARE : (plane + 1) * SHARE]
        clean = (latent[:, plane, :] - noise_now * value) / root_now
        guided[:, plane, :] = value
        stepped[:, plane, :] = root_next * clean + noise_next * value


def final_call(roots, pieces, latent):
    shape = jax.ShapeDtypeStruct((LAT, DEP_DEV, SHARE), F32)
    return pl.pallas_call(
        final_kernel,
        out_shape=(shape, shape),
        in_specs=[VMEM, VMEM, VMEM],
        out_specs=(VMEM, VMEM),
        compiler_params=params(2),
        name="final",
    )(roots, pieces, latent)


def plan(step_value):
    frac = (step_value / 1000.0 + 0.008) / 1.008
    return jnp.cos(frac * math.pi / 2.0) ** 2


EVEN_PAIRS = [(at, at ^ 1) for at in range(SLABS)]
ODD_PAIRS = [(at, ((at + 1) ^ 1) - 1) for at in range(1, SLABS - 1)]


def per_device(
    features,
    latent,
    cond_codes,
    guide_codes,
    timestep,
    code_table,
    time_weight,
    film_weight,
    conv_one,
    conv_two,
    head_weight,
):
    planes = features.reshape(DEP_DEV, HW, C)
    time_value = timestep[0].astype(F32)
    half_width = EMB // 2
    frequency = jnp.exp(-math.log(10000.0) * jnp.arange(half_width, dtype=F32) / half_width)
    angles = time_value * frequency
    sinus = jnp.concatenate([jnp.cos(angles), jnp.sin(angles)]).reshape(1, EMB)
    now_bar = plan(time_value)
    next_bar = plan(time_value - STRIDE)
    roots = jnp.sqrt(jnp.stack([1.0 - now_bar, now_bar, next_bar, 1.0 - next_bar]))
    roots = jnp.repeat(roots, C // 4).reshape(1, C)

    odd, even = rims_call(planes)
    odd = lax.ppermute(odd, "slab", ODD_PAIRS)
    stats = stats_call(planes)
    every = lax.all_to_all(stats, "slab", 0, 0)
    even = lax.ppermute(even, "slab", EVEN_PAIRS)
    mod, base, mix, roots = prep_call(
        cond_codes,
        guide_codes,
        sinus,
        roots,
        code_table,
        time_weight,
        film_weight,
        conv_two.reshape(TAPS * C, C),
        head_weight.T,
        planes,
    )
    weight = conv_one.reshape(TAPS * C, C)
    inner, norm = inner_call(every, planes, weight, odd)
    first, stats, odd, even = outer_call(norm, odd, even, inner, weight)
    odd = lax.ppermute(odd, "slab", ODD_PAIRS)
    every = lax.all_to_all(stats, "slab", 0, 0)
    even = lax.ppermute(even, "slab", EVEN_PAIRS)
    near, norm = near_call(every, first, mod, mix, odd)
    pieces = head_call(norm, odd, even, near, base, mix)
    pieces = lax.all_to_all(pieces, "cond", 0, 0)
    return final_call(roots, pieces, latent)


def solution(mesh):
    placed = (
        P("cond", "slab", None, None, None),
        P(None, "slab", "cond"),
        P("cond", None),
        P(),
        P(),
        P(),
        P(),
        P(),
        P(),
        P(),
        P(),
    )
    return jax.shard_map(
        per_device,
        mesh=mesh,
        in_specs=placed,
        out_specs=(P(None, "slab", "cond"), P(None, "slab", "cond")),
        check_vma=False,
    )
```

```python
import math

import jax
import jax.numpy as jnp
from jax import lax
from jax.experimental import pallas as pl
from jax.experimental.pallas import tpu as pltpu
from jax.sharding import PartitionSpec as P

C = 128
GROUPS = 32
PER_GROUP = C // GROUPS
EMB = 256
LAT = 4
SLOTS = 8
CODES = 16
STRIDE = 20
DEP_DEV = 2
H = 16
W = 64
HW = H * W
TERMS = 16
SHARE = HW // TERMS
SLABS = 16
CELLS = DEP_DEV * HW
MEMBERS = float(SLABS * CELLS * PER_GROUP)
TAPS = 27
F32 = jnp.float32
BF16 = jnp.bfloat16
ROWS = 2 * LAT

VMEM = pl.BlockSpec(memory_space=pltpu.VMEM)


def params(mebibytes):
    return pltpu.CompilerParams(vmem_limit_bytes=mebibytes * 1024 * 1024)


def cost(gigaflops, mebibytes):
    return pl.CostEstimate(
        flops=gigaflops * 10**9, bytes_accessed=mebibytes * 2**20, transcendentals=0
    )


def dot_last(left, right):
    return lax.dot_general(left, right, (((1,), (1,)), ((), ())), preferred_element_type=F32)


def silu(values):
    half = 0.5 * values
    return half + half * jnp.tanh(half)


def column_sum(values):
    partial = jnp.sum(values.reshape(-1, W, C), axis=0)
    return jnp.sum(partial, axis=0, keepdims=True)


def own_stats(values, out_ref):
    pivot = jnp.sum(values[:W], axis=0, keepdims=True) * (1.0 / W)
    apart = values - pivot
    total = column_sum(apart)
    square = column_sum(apart * apart) - total * total * (1.0 / CELLS)
    both = jnp.concatenate([total + CELLS * pivot, square], axis=0)
    out_ref[...] = jnp.broadcast_to(both[None], (SLABS, 2, C))


def over_group(values):
    lane = lax.broadcasted_iota(jnp.int32, values.shape, 1)
    for step in (1, 2):
        other = jnp.where(
            lane // step % 2 == 0, pltpu.roll(values, C - step, 1), pltpu.roll(values, step, 1)
        )
        values = values + other
    return values


def three_parts(values):
    high = values.astype(BF16).astype(F32)
    rest = values - high
    middle = rest.astype(BF16).astype(F32)
    low = rest - middle
    zero = jnp.zeros_like(values)
    return jnp.concatenate([high, middle, low, zero], axis=0).astype(BF16)


def all_stats(every_ref):
    every = every_ref[...]
    totals = every[:, 0, :]
    squares = every[:, 1, :]
    average = over_group(jnp.sum(totals, axis=0, keepdims=True)) / MEMBERS
    apart = totals * (1.0 / CELLS) - average
    spread = (
        over_group(jnp.sum(squares + CELLS * (apart * apart), axis=0, keepdims=True))
        / MEMBERS
    )
    return average, 1.0 / jnp.sqrt(spread + 1e-05)


def stats_kernel(features, out):
    own_stats(features[...].reshape(CELLS, C).astype(F32), out)


def stats_call(features):
    return pl.pallas_call(
        stats_kernel,
        out_shape=jax.ShapeDtypeStruct((SLABS, 2, C), F32),
        in_specs=[VMEM],
        out_specs=VMEM,
        compiler_params=params(4),
        cost_estimate=cost(2, 1),
        name="stats",
    )(features)


def rims_kernel(planes, step, even, odd, time):
    time[...] = jnp.broadcast_to(step[...].astype(F32).reshape(1, 1), (8, C))
    parity = lax.axis_index("slab") % 2
    even[...] = planes[DEP_DEV - 1 - parity]
    odd[...] = planes[parity]


def rims_call(planes, step):
    plane = jax.ShapeDtypeStruct((HW, C), BF16)
    return pl.pallas_call(
        rims_kernel,
        out_shape=(plane, plane, jax.ShapeDtypeStruct((8, C), F32)),
        in_specs=[VMEM, VMEM],
        out_specs=(VMEM, VMEM, VMEM),
        compiler_params=params(4),
        cost_estimate=cost(2, 1),
        name="rims",
    )(planes, step)


def exact(left, right):
    parts = three_parts(left)
    coarse = right.astype(BF16)
    fine = (right - coarse.astype(F32)).astype(BF16)
    product = jnp.dot(parts, coarse, preferred_element_type=F32) + jnp.dot(
        parts, fine, preferred_element_type=F32
    )
    return three_sum(product)


def plan(step_value):
    frac = (step_value / 1000.0 + 0.008) / 1.008
    return jnp.cos(frac * (math.pi / 2.0)) ** 2


def sampler_roots(time_value):
    now_bar = plan(time_value)
    next_bar = plan(time_value - STRIDE)
    return jnp.sqrt(
        jnp.concatenate([1.0 - now_bar, now_bar, next_bar, 1.0 - next_bar], axis=0)
    )


def modulate(time_value, codes, table, time_weight, film):
    lane = lax.broadcasted_iota(jnp.int32, (1, EMB // 2), 1)
    angles = time_value * jnp.exp(
        -math.log(10000.0) * lane.astype(F32) / (EMB // 2)
    )
    sinus = jnp.concatenate([jnp.cos(angles), jnp.sin(angles)], axis=1)
    wanted = jnp.zeros((1, SLOTS * CODES), jnp.int32)
    for slot in range(SLOTS):
        wanted = jnp.where(lane // CODES == slot, codes[0:1, slot : slot + 1], wanted)
    one_hot = (lane % CODES == wanted).astype(F32)
    rows = jnp.broadcast_to(jnp.concatenate([sinus, one_hot], axis=1), (8, EMB + SLOTS * CODES))
    tables = jnp.concatenate([time_weight[...], table[...]], axis=0)
    embedding = silu(exact(rows, tables))
    return exact(embedding, film[...])[:1]


def own_weight(guides):
    term = lax.axis_index("cond")
    lane = lax.broadcasted_iota(jnp.int32, (1, TERMS), 1)
    values = guides[...].astype(F32)
    others = jnp.sum(jnp.where(lane == 0, 0.0, values), axis=1, keepdims=True)
    mine = jnp.sum(jnp.where(lane == term, values, 0.0), axis=1, keepdims=True)
    return jnp.where(term == 0, TERMS - others, mine) * (1.0 / 16.0)


def three_sum(product):
    return product[:ROWS] + (product[ROWS : 2 * ROWS] + product[2 * ROWS : 3 * ROWS])


def compose(conv_two, head, weight):
    head_rows = jnp.concatenate([head[...], head[...]], axis=0)
    upper = lax.broadcasted_iota(jnp.int32, (ROWS, C), 0) < LAT
    composed = three_sum(dot_last(three_parts(head_rows), conv_two[...])) * weight
    nothing = jnp.zeros((ROWS, C), F32)
    rows = []
    for near in range(9):
        blocks = []
        for plane in range(DEP_DEV + 2):
            at = [
                composed[:, (tap * 9 + near) * C : (tap * 9 + near + 1) * C]
                if 0 <= tap < 3
                else nothing
                for tap in (plane, plane - 1)
            ]
            blocks.append(jnp.where(upper, at[0], at[1]))
        rows.append(jnp.concatenate(blocks, axis=1))
    return jnp.concatenate(rows, axis=0)


def direct(features, head, weight):
    head_rows = jnp.concatenate([head[...], head[...]], axis=0)
    upper = lax.broadcasted_iota(jnp.int32, (ROWS, C), 0) < LAT
    wide = jnp.concatenate(
        [jnp.where(upper, head_rows, 0.0), jnp.where(upper, 0.0, head_rows)], axis=1
    )
    both = jnp.concatenate([features[0], features[1]], axis=1)
    return three_sum(dot_last(three_parts(wide), both)) * weight


def conv_part(planes, taps_of, weight, held, side):
    held[0:W, :] = jnp.zeros((W, len(planes) * C), BF16)
    held[W + HW :, :] = jnp.zeros((W, len(planes) * C), BF16)
    for at, values in enumerate(planes):
        held[W : W + HW, at * C : (at + 1) * C] = values.astype(BF16)
    zero = jnp.zeros((C, C), BF16)
    depth = len(planes) * C

    def block(tap, row, col):
        at = ((tap * 3 + row) * 3 + col) * C
        return weight[at : at + C, :]

    products = []
    for col in range(3):
        right = jnp.concatenate(
            [
                jnp.concatenate(
                    [zero if tap is None else block(tap, row, col) for tap in taps], axis=1
                )
                for row in range(3)
                for taps in taps_of
            ],
            axis=0,
        )
        products.append(
            sum(
                jnp.dot(
                    held[row * W : row * W + HW, :],
                    right[row * depth : (row + 1) * depth],
                    preferred_element_type=F32,
                )
                for row in range(3)
            )
        )
    column = lax.broadcasted_iota(jnp.int32, (HW, C), 0) % W
    sums = []
    for plane in range(DEP_DEV):
        part = [product[:, plane * C : (plane + 1) * C] for product in products]
        side[8 : 8 + HW, :] = part[0]
        before = jnp.where(column == 0, 0.0, side[7 : 7 + HW, :])
        side[8 : 8 + HW, :] = part[2]
        after = jnp.where(column == W - 1, 0.0, side[9 : 9 + HW, :])
        sums.append(part[1] + before + after)
    return sums


def conv_scratch():
    return [pltpu.VMEM((HW + 2 * W, 4 * C), BF16), pltpu.VMEM((HW + 16, C), F32)]


def rim_planes(swapped):
    slab = lax.axis_index("slab")
    first = slab % 2 == 0
    low = jnp.where(first, swapped[1], swapped[0])
    high = jnp.where(first, swapped[0], swapped[1])
    return [jnp.where(slab > 0, low, 0.0), jnp.where(slab < SLABS - 1, high, 0.0)]


def conv_kernel(every, even, odd, own, weight, out, out_stats, out_even, out_odd, held, side):
    average, scale = all_stats(every)
    shift = -average * scale

    def act(values):
        return silu(values.astype(F32) * scale + shift)

    low, high = rim_planes([act(even[...]), act(odd[...])])
    planes = [low, act(own[0]), act(own[1]), high]
    sums = conv_part(planes, [(0, None), (1, 0), (2, 1), (None, 2)], weight, held, side)
    for at in range(DEP_DEV):
        out[at] = sums[at]
    own_stats(out[...].reshape(CELLS, C), out_stats)
    parity = lax.axis_index("slab") % 2
    out_even[...] = out[DEP_DEV - 1 - parity].astype(BF16)
    out_odd[...] = out[parity].astype(BF16)


def conv_call(every, even, odd, own, weight):
    plane = jax.ShapeDtypeStruct((HW, C), BF16)
    return pl.pallas_call(
        conv_kernel,
        out_shape=(
            jax.ShapeDtypeStruct((DEP_DEV, HW, C), F32),
            jax.ShapeDtypeStruct((SLABS, 2, C), F32),
            plane,
            plane,
        ),
        in_specs=[VMEM] * 5,
        out_specs=(VMEM,) * 4,
        scratch_shapes=conv_scratch(),
        compiler_params=params(16),
        cost_estimate=cost(2, 32),
        name="conv",
    )(every, even, odd, own, weight)


def mixed(planes, weights, held):
    for at, values in enumerate(planes):
        held[:, at * C : (at + 1) * C] = values.astype(BF16)
    coarse = weights.astype(BF16).astype(F32)
    pair = jnp.concatenate([coarse, weights - coarse], axis=0).astype(BF16)
    product = dot_last(pair, held[...])
    return product[: 9 * ROWS] + product[9 * ROWS :]


def head_kernel(
    every,
    even,
    odd,
    own,
    features,
    time,
    codes,
    guides,
    table,
    time_weight,
    film,
    conv_two,
    head,
    out,
    roots,
    held,
):
    time_value = time[0:1, :]
    roots[...] = sampler_roots(time_value)
    mod = modulate(time_value, codes, table, time_weight, film)
    weight = own_weight(guides)
    mix = compose(conv_two, head, weight)
    base = direct(features, head, weight)
    average, scale = all_stats(every)
    factor = scale * (1.0 + mod[:, :C])
    shift = mod[:, C:] - average * factor

    def act(values):
        return silu(values.astype(F32) * factor + shift)

    low, high = rim_planes([act(even[...]), act(odd[...])])
    product = mixed([low, act(own[0]), act(own[1]), high], mix, held)
    at = lax.broadcasted_iota(jnp.int32, (ROWS, HW), 1)
    summed = base
    for col in range(3):
        part = [product[(row * 3 + col) * ROWS : (row * 3 + col + 1) * ROWS] for row in range(3)]
        values = (
            part[1]
            + jnp.where(at < W, 0.0, pltpu.roll(part[0], W, 1))
            + jnp.where(at >= HW - W, 0.0, pltpu.roll(part[2], HW - W, 1))
        )
        if col == 0:
            values = jnp.where(at % W == 0, 0.0, pltpu.roll(values, 1, 1))
        if col == 2:
            values = jnp.where(at % W == W - 1, 0.0, pltpu.roll(values, HW - 1, 1))
        summed = summed + values
    for target in range(TERMS):
        piece = summed[:, target * SHARE : (target + 1) * SHARE]
        out[target] = jnp.concatenate([piece[:LAT], piece[LAT:]], axis=1)


def head_call(*operands):
    return pl.pallas_call(
        head_kernel,
        out_shape=(
            jax.ShapeDtypeStruct((TERMS, LAT, DEP_DEV * SHARE), F32),
            jax.ShapeDtypeStruct((4, C), F32),
        ),
        in_specs=[VMEM] * len(operands),
        out_specs=(VMEM, VMEM),
        scratch_shapes=[pltpu.VMEM((HW, 4 * C), BF16)],
        compiler_params=params(12),
        cost_estimate=cost(1, 32),
        name="head",
    )(*operands)


def final_kernel(roots, pieces, latent, guided, stepped):
    total = jnp.sum(pieces[...], axis=0)
    noise_now, root_now, root_next, noise_next = [roots[at : at + 1, :SHARE] for at in range(4)]
    for plane in range(DEP_DEV):
        value = total[:, plane * SHARE : (plane + 1) * SHARE]
        clean = (latent[:, plane, :] - noise_now * value) / root_now
        guided[:, plane, :] = value
        stepped[:, plane, :] = root_next * clean + noise_next * value


def final_call(roots, pieces, latent):
    shape = jax.ShapeDtypeStruct((LAT, DEP_DEV, SHARE), F32)
    return pl.pallas_call(
        final_kernel,
        out_shape=(shape, shape),
        in_specs=[VMEM, VMEM, VMEM],
        out_specs=(VMEM, VMEM),
        compiler_params=params(2),
        name="final",
    )(roots, pieces, latent)


EVEN_PAIRS = [(at, at ^ 1) for at in range(SLABS)]
ODD_PAIRS = [(at, ((at + 1) ^ 1) - 1) for at in range(1, SLABS - 1)]


def per_device(
    features,
    latent,
    cond_codes,
    guide_codes,
    timestep,
    code_table,
    time_weight,
    film_weight,
    conv_one,
    conv_two,
    head_weight,
):
    planes = features.reshape(DEP_DEV, HW, C)
    even, odd, time = rims_call(planes, timestep)
    even = lax.ppermute(even, "slab", EVEN_PAIRS)
    odd = lax.ppermute(odd, "slab", ODD_PAIRS)
    every = lax.all_to_all(stats_call(planes), "slab", 0, 0)
    first, stats, even, odd = conv_call(
        every, even, odd, planes, conv_one.reshape(TAPS * C, C)
    )
    even = lax.ppermute(even, "slab", EVEN_PAIRS)
    odd = lax.ppermute(odd, "slab", ODD_PAIRS)
    every = lax.all_to_all(stats, "slab", 0, 0)
    pieces, roots = head_call(
        every,
        even,
        odd,
        first,
        planes,
        time,
        cond_codes,
        guide_codes.reshape(1, TERMS),
        code_table.reshape(SLOTS * CODES, EMB),
        time_weight,
        film_weight,
        conv_two.reshape(TAPS * C, C),
        head_weight.T,
    )
    pieces = lax.all_to_all(pieces, "cond", 0, 0)
    return final_call(roots, pieces, latent)


def solution(mesh):
    placed = (
        P("cond", "slab", None, None, None),
        P(None, "slab", "cond"),
        P("cond", None),
        P(),
        P(),
        P(),
        P(),
        P(),
        P(),
        P(),
        P(),
    )
    return jax.shard_map(
        per_device,
        mesh=mesh,
        in_specs=placed,
        out_specs=(P(None, "slab", "cond"), P(None, "slab", "cond")),
        check_vma=False,
    )
```

```python
import math

import jax
import jax.numpy as jnp
from jax import lax
from jax.experimental import pallas as pl
from jax.experimental.pallas import tpu as pltpu
from jax.sharding import PartitionSpec as P

C = 128
GROUPS = 32
PER_GROUP = C // GROUPS
EMB = 256
LAT = 4
SLOTS = 8
CODES = 16
STRIDE = 20
DEP_DEV = 2
H = 16
W = 64
HW = H * W
TERMS = 16
SHARE = HW // TERMS
SLABS = 16
CELLS = DEP_DEV * HW
MEMBERS = float(SLABS * CELLS * PER_GROUP)
TAPS = 27
F32 = jnp.float32
BF16 = jnp.bfloat16
ROWS = 2 * LAT

VMEM = pl.BlockSpec(memory_space=pltpu.VMEM)


def params(mebibytes):
    return pltpu.CompilerParams(vmem_limit_bytes=mebibytes * 1024 * 1024)


def cost(gigaflops, mebibytes):
    return pl.CostEstimate(
        flops=gigaflops * 10**9, bytes_accessed=mebibytes * 2**20, transcendentals=0
    )


def dot_last(left, right):
    return lax.dot_general(left, right, (((1,), (1,)), ((), ())), preferred_element_type=F32)


def silu(values):
    half = 0.5 * values
    return half + half * jnp.tanh(half)


def column_sum(values):
    partial = jnp.sum(values.reshape(-1, W, C), axis=0)
    return jnp.sum(partial, axis=0, keepdims=True)


def own_stats(values, out_ref):
    pivot = jnp.sum(values[:W], axis=0, keepdims=True) * (1.0 / W)
    apart = values - pivot
    total = column_sum(apart)
    square = column_sum(apart * apart) - total * total * (1.0 / CELLS)
    both = jnp.concatenate([total + CELLS * pivot, square], axis=0)
    out_ref[...] = jnp.broadcast_to(both[None], (SLABS, 2, C))


def over_group(values):
    lane = lax.broadcasted_iota(jnp.int32, values.shape, 1)
    for step in (1, 2):
        other = jnp.where(
            lane // step % 2 == 0, pltpu.roll(values, C - step, 1), pltpu.roll(values, step, 1)
        )
        values = values + other
    return values


def three_parts(values):
    high = values.astype(BF16).astype(F32)
    rest = values - high
    middle = rest.astype(BF16).astype(F32)
    low = rest - middle
    zero = jnp.zeros_like(values)
    return jnp.concatenate([high, middle, low, zero], axis=0).astype(BF16)


def all_stats(every_ref):
    every = every_ref[...]
    totals = every[:, 0, :]
    squares = every[:, 1, :]
    average = over_group(jnp.sum(totals, axis=0, keepdims=True)) / MEMBERS
    apart = totals * (1.0 / CELLS) - average
    spread = (
        over_group(jnp.sum(squares + CELLS * (apart * apart), axis=0, keepdims=True))
        / MEMBERS
    )
    return average, 1.0 / jnp.sqrt(spread + 1e-05)


def stats_kernel(features, step, out, time):
    time[...] = jnp.broadcast_to(step[...].astype(F32).reshape(1, 1), (8, C))
    own_stats(features[...].reshape(CELLS, C).astype(F32), out)


def stats_call(features, step):
    return pl.pallas_call(
        stats_kernel,
        out_shape=(
            jax.ShapeDtypeStruct((SLABS, 2, C), F32),
            jax.ShapeDtypeStruct((8, C), F32),
        ),
        in_specs=[VMEM, VMEM],
        out_specs=(VMEM, VMEM),
        compiler_params=params(4),
        cost_estimate=cost(4, 1),
        name="stats",
    )(features, step)


def exact(left, right):
    parts = three_parts(left)
    coarse = right.astype(BF16)
    fine = (right - coarse.astype(F32)).astype(BF16)
    product = jnp.dot(parts, coarse, preferred_element_type=F32) + jnp.dot(
        parts, fine, preferred_element_type=F32
    )
    return three_sum(product)


def plan(step_value):
    frac = (step_value / 1000.0 + 0.008) / 1.008
    return jnp.cos(frac * (math.pi / 2.0)) ** 2


def sampler_roots(time_value):
    now_bar = plan(time_value)
    next_bar = plan(time_value - STRIDE)
    return jnp.sqrt(
        jnp.concatenate([1.0 - now_bar, now_bar, next_bar, 1.0 - next_bar], axis=0)
    )


def modulate(time_value, codes, table, time_weight, film):
    lane = lax.broadcasted_iota(jnp.int32, (1, EMB // 2), 1)
    angles = time_value * jnp.exp(
        -math.log(10000.0) * lane.astype(F32) / (EMB // 2)
    )
    sinus = jnp.concatenate([jnp.cos(angles), jnp.sin(angles)], axis=1)
    wanted = jnp.zeros((1, SLOTS * CODES), jnp.int32)
    for slot in range(SLOTS):
        wanted = jnp.where(lane // CODES == slot, codes[0:1, slot : slot + 1], wanted)
    one_hot = (lane % CODES == wanted).astype(F32)
    rows = jnp.broadcast_to(jnp.concatenate([sinus, one_hot], axis=1), (8, EMB + SLOTS * CODES))
    tables = jnp.concatenate([time_weight[...], table[...]], axis=0)
    embedding = silu(exact(rows, tables))
    return exact(embedding, film[...])[:1]


def own_weight(guides):
    term = lax.axis_index("cond")
    lane = lax.broadcasted_iota(jnp.int32, (1, TERMS), 1)
    values = guides
    others = jnp.sum(jnp.where(lane == 0, 0.0, values), axis=1, keepdims=True)
    mine = jnp.sum(jnp.where(lane == term, values, 0.0), axis=1, keepdims=True)
    return jnp.where(term == 0, TERMS - others, mine) * (1.0 / 16.0)


def three_sum(product):
    return product[:ROWS] + (product[ROWS : 2 * ROWS] + product[2 * ROWS : 3 * ROWS])


def compose(conv_two, head, weight):
    head_rows = jnp.concatenate([head, head], axis=0)
    upper = lax.broadcasted_iota(jnp.int32, (ROWS, C), 0) < LAT
    composed = three_sum(dot_last(three_parts(head_rows), conv_two[...])) * weight
    nothing = jnp.zeros((ROWS, C), F32)
    rows = []
    for near in range(9):
        blocks = []
        for plane in range(DEP_DEV + 2):
            at = [
                composed[:, (tap * 9 + near) * C : (tap * 9 + near + 1) * C]
                if 0 <= tap < 3
                else nothing
                for tap in (plane, plane - 1)
            ]
            blocks.append(jnp.where(upper, at[0], at[1]))
        rows.append(jnp.concatenate(blocks, axis=1))
    return jnp.concatenate(rows, axis=0)


def direct(features, head, weight):
    head_rows = jnp.concatenate([head, head], axis=0)
    upper = lax.broadcasted_iota(jnp.int32, (ROWS, C), 0) < LAT
    wide = jnp.concatenate(
        [jnp.where(upper, head_rows, 0.0), jnp.where(upper, 0.0, head_rows)], axis=1
    )
    both = jnp.concatenate([features[0], features[1]], axis=1)
    return three_sum(dot_last(three_parts(wide), both)) * weight


def rim_planes(swapped):
    slab = lax.axis_index("slab")
    first = slab % 2 == 0
    low = jnp.where(first, swapped[1], swapped[0])
    high = jnp.where(first, swapped[0], swapped[1])
    return [jnp.where(slab > 0, low, 0.0), jnp.where(slab < SLABS - 1, high, 0.0)]


def store_planes(held, planes):
    held[0:W, :] = jnp.zeros((W, held.shape[1]), BF16)
    held[W + HW :, :] = jnp.zeros((W, held.shape[1]), BF16)
    for at, values in enumerate(planes):
        held[W : W + HW, at * C : (at + 1) * C] = values.astype(BF16)


def block(weight, tap, row, col):
    at = ((tap * 3 + row) * 3 + col) * C
    return weight[at : at + C, :]


def shifted_sum(part, side):
    column = lax.broadcasted_iota(jnp.int32, (HW, C), 0) % W
    side[8 : 8 + HW, :] = part[0]
    before = jnp.where(column == 0, 0.0, side[7 : 7 + HW, :])
    side[8 : 8 + HW, :] = part[2]
    after = jnp.where(column == W - 1, 0.0, side[9 : 9 + HW, :])
    return part[1] + before + after


def conv_kernel(every, even, odd, own, weight, out, out_stats, held, norm, side):
    average, scale = all_stats(every)
    shift = -average * scale
    norm[0:1, :] = scale
    norm[1:2, :] = shift

    def act(values):
        return silu(values.astype(F32) * scale + shift)

    parity = lax.axis_index("slab") % 2
    low, high = rim_planes([act(even[parity]), act(odd[1 - parity])])
    store_planes(held, [low, act(own[0]), act(own[1]), high])
    zero = jnp.zeros((C, C), BF16)
    products = []
    for col in range(3):
        product = None
        for row in range(3):
            right = jnp.concatenate(
                [
                    jnp.concatenate(
                        [
                            zero if tap is None else block(weight, tap, row, col)
                            for tap in taps
                        ],
                        axis=1,
                    )
                    for taps in [(0, None), (1, 0), (2, 1), (None, 2)]
                ],
                axis=0,
            )
            term = jnp.dot(
                held[row * W : row * W + HW, :], right, preferred_element_type=F32
            )
            product = term if product is None else product + term
        products.append(product)
    for plane in range(DEP_DEV):
        out[plane] = shifted_sum(
            [product[:, plane * C : (plane + 1) * C] for product in products], side
        )
    own_stats(out[...].reshape(CELLS, C), out_stats)


def conv_call(*operands):
    return pl.pallas_call(
        conv_kernel,
        out_shape=(
            jax.ShapeDtypeStruct((DEP_DEV, HW, C), F32),
            jax.ShapeDtypeStruct((SLABS, 2, C), F32),
            jax.ShapeDtypeStruct((HW + 2 * W, 4 * C), BF16),
            jax.ShapeDtypeStruct((8, C), F32),
        ),
        in_specs=[VMEM] * len(operands),
        out_specs=(VMEM,) * 4,
        scratch_shapes=[pltpu.VMEM((HW + 16, C), F32)],
        compiler_params=params(16),
        cost_estimate=cost(2, 32),
        name="conv",
    )(*operands)


def far_planes(norm, even, odd, near, weight, held, side):
    def act(values):
        return silu(values.astype(F32) * norm[0:1, :] + norm[1:2, :])

    parity = lax.axis_index("slab") % 2
    store_planes(held, rim_planes([act(even[1 - parity]), act(odd[parity])]))
    planes = []
    for plane in range(2):
        left = []
        for row in range(3):
            rows = pl.ds(row * W, HW)
            if plane == 0:
                left += [held[rows, :C], near[rows, : 2 * C]]
            else:
                left += [near[rows, 2 * C :], held[rows, C:]]
        left = jnp.concatenate(left, axis=1)

        def right(col):
            return jnp.concatenate(
                [block(weight, tap, row, col) for row in range(3) for tap in range(3)], axis=0
            )

        pair = jnp.concatenate([right(0), right(1)], axis=1)
        wide = jnp.dot(left, pair, preferred_element_type=F32)
        narrow = jnp.dot(left, right(2), preferred_element_type=F32)
        planes.append(shifted_sum([wide[:, :C], wide[:, C:], narrow], side))
    return planes


def mixed(planes, weights, held):
    for at, values in enumerate(planes):
        held[:, at * C : (at + 1) * C] = values.astype(BF16)
    coarse = weights.astype(BF16).astype(F32)
    pair = jnp.concatenate([coarse, weights - coarse], axis=0).astype(BF16)
    product = dot_last(pair, held[...])
    return product[: 9 * ROWS] + product[9 * ROWS :]


def head_kernel(
    every,
    first,
    norm,
    even,
    odd,
    near,
    weight,
    own,
    time,
    codes,
    guides,
    table,
    time_weight,
    film,
    conv_two,
    head,
    out,
    roots,
    rim,
    side,
    held,
):
    far = far_planes(norm, even, odd, near, weight, rim, side)
    time_value = time[0:1, :]
    roots[...] = sampler_roots(time_value)
    mod = modulate(time_value, codes, table, time_weight, film)
    share = own_weight(guides[...].astype(F32))
    mix = compose(conv_two, head[...], share)
    base = direct(own, head[...], share)
    average, scale = all_stats(every)
    factor = scale * (1.0 + mod[:, :C])
    shift = mod[:, C:] - average * factor

    def act(values):
        return silu(values * factor + shift)

    slab = lax.axis_index("slab")
    low = jnp.where(slab > 0, act(far[0]), 0.0)
    high = jnp.where(slab < SLABS - 1, act(far[1]), 0.0)
    product = mixed([low, act(first[0]), act(first[1]), high], mix, held)
    at = lax.broadcasted_iota(jnp.int32, (ROWS, HW), 1)
    summed = base
    for col in range(3):
        part = [product[(row * 3 + col) * ROWS : (row * 3 + col + 1) * ROWS] for row in range(3)]
        values = (
            part[1]
            + jnp.where(at < W, 0.0, pltpu.roll(part[0], W, 1))
            + jnp.where(at >= HW - W, 0.0, pltpu.roll(part[2], HW - W, 1))
        )
        if col == 0:
            values = jnp.where(at % W == 0, 0.0, pltpu.roll(values, 1, 1))
        if col == 2:
            values = jnp.where(at % W == W - 1, 0.0, pltpu.roll(values, HW - 1, 1))
        summed = summed + values
    for target in range(TERMS):
        piece = summed[:, target * SHARE : (target + 1) * SHARE]
        out[target] = jnp.concatenate([piece[:LAT], piece[LAT:]], axis=1)


def head_call(*operands):
    return pl.pallas_call(
        head_kernel,
        out_shape=(
            jax.ShapeDtypeStruct((TERMS, LAT, DEP_DEV * SHARE), F32),
            jax.ShapeDtypeStruct((4, C), F32),
        ),
        in_specs=[VMEM] * len(operands),
        out_specs=(VMEM, VMEM),
        scratch_shapes=[
            pltpu.VMEM((HW + 2 * W, 2 * C), BF16),
            pltpu.VMEM((HW + 16, C), F32),
            pltpu.VMEM((HW, 4 * C), BF16),
        ],
        compiler_params=params(20),
        cost_estimate=cost(1, 32),
        name="head",
    )(*operands)


def final_kernel(roots, pieces, latent, guided, stepped):
    total = jnp.sum(pieces[...], axis=0)
    noise_now, root_now, root_next, noise_next = [roots[at : at + 1, :SHARE] for at in range(4)]
    for plane in range(DEP_DEV):
        value = total[:, plane * SHARE : (plane + 1) * SHARE]
        clean = (latent[:, plane, :] - noise_now * value) / root_now
        guided[:, plane, :] = value
        stepped[:, plane, :] = root_next * clean + noise_next * value


def final_call(roots, pieces, latent):
    shape = jax.ShapeDtypeStruct((LAT, DEP_DEV, SHARE), F32)
    return pl.pallas_call(
        final_kernel,
        out_shape=(shape, shape),
        in_specs=[VMEM, VMEM, VMEM],
        out_specs=(VMEM, VMEM),
        compiler_params=params(2),
        name="final",
    )(roots, pieces, latent)


EVEN_PAIRS = [(at, at ^ 1) for at in range(SLABS)]
ODD_PAIRS = [(at, ((at + 1) ^ 1) - 1) for at in range(1, SLABS - 1)]


def per_device(
    features,
    latent,
    cond_codes,
    guide_codes,
    timestep,
    code_table,
    time_weight,
    film_weight,
    conv_one,
    conv_two,
    head_weight,
):
    planes = features.reshape(DEP_DEV, HW, C)
    even = lax.ppermute(planes, "slab", EVEN_PAIRS)
    odd = lax.ppermute(planes, "slab", ODD_PAIRS)
    stats, time = stats_call(planes, timestep)
    every = lax.all_to_all(stats, "slab", 0, 0)
    weight = conv_one.reshape(TAPS * C, C)
    first, stats, near, norm = conv_call(every, even, odd, planes, weight)
    every = lax.all_to_all(stats, "slab", 0, 0)
    pieces, roots = head_call(
        every,
        first,
        norm,
        even,
        odd,
        near,
        weight,
        planes,
        time,
        cond_codes,
        guide_codes.reshape(1, TERMS),
        code_table.reshape(SLOTS * CODES, EMB),
        time_weight,
        film_weight,
        conv_two.reshape(TAPS * C, C),
        head_weight.T,
    )
    pieces = lax.all_to_all(pieces, "cond", 0, 0)
    return final_call(roots, pieces, latent)


def solution(mesh):
    placed = (
        P("cond", "slab", None, None, None),
        P(None, "slab", "cond"),
        P("cond", None),
        P(),
        P(),
        P(),
        P(),
        P(),
        P(),
        P(),
        P(),
    )
    return jax.shard_map(
        per_device,
        mesh=mesh,
        in_specs=placed,
        out_specs=(P(None, "slab", "cond"), P(None, "slab", "cond")),
        check_vma=False,
    )
```

```python
import math

import jax
import jax.numpy as jnp
from jax import lax
from jax.experimental import pallas as pl
from jax.experimental.pallas import tpu as pltpu
from jax.sharding import PartitionSpec as P

C = 128
GROUPS = 32
PER_GROUP = C // GROUPS
EMB = 256
LAT = 4
SLOTS = 8
CODES = 16
STRIDE = 20
DEP_DEV = 2
H = 16
W = 64
HW = H * W
TERMS = 16
SHARE = HW // TERMS
SLABS = 16
CELLS = DEP_DEV * HW
MEMBERS = float(SLABS * CELLS * PER_GROUP)
TAPS = 27
F32 = jnp.float32
BF16 = jnp.bfloat16
ROWS = 2 * LAT

VMEM = pl.BlockSpec(memory_space=pltpu.VMEM)


def params(mebibytes):
    return pltpu.CompilerParams(vmem_limit_bytes=mebibytes * 1024 * 1024)


def cost(gigaflops, mebibytes):
    return pl.CostEstimate(
        flops=gigaflops * 10**9, bytes_accessed=mebibytes * 2**20, transcendentals=0
    )


def dot_last(left, right):
    return lax.dot_general(left, right, (((1,), (1,)), ((), ())), preferred_element_type=F32)


def silu(values):
    half = 0.5 * values
    return half + half * jnp.tanh(half)


def column_sum(values):
    partial = jnp.sum(values.reshape(-1, W, C), axis=0)
    return jnp.sum(partial, axis=0, keepdims=True)


def own_stats(values, out_ref):
    pivot = jnp.sum(values[:W], axis=0, keepdims=True) * (1.0 / W)
    apart = values - pivot
    total = column_sum(apart)
    square = column_sum(apart * apart) - total * total * (1.0 / CELLS)
    both = jnp.concatenate([total + CELLS * pivot, square], axis=0)
    out_ref[...] = jnp.broadcast_to(both[None], (SLABS, 2, C))


def over_group(values):
    lane = lax.broadcasted_iota(jnp.int32, values.shape, 1)
    for step in (1, 2):
        other = jnp.where(
            lane // step % 2 == 0, pltpu.roll(values, C - step, 1), pltpu.roll(values, step, 1)
        )
        values = values + other
    return values


def three_parts(values):
    high = values.astype(BF16).astype(F32)
    rest = values - high
    middle = rest.astype(BF16).astype(F32)
    low = rest - middle
    zero = jnp.zeros_like(values)
    return jnp.concatenate([high, middle, low, zero], axis=0).astype(BF16)


def all_stats(every_ref):
    every = every_ref[...]
    totals = every[:, 0, :]
    squares = every[:, 1, :]
    average = over_group(jnp.sum(totals, axis=0, keepdims=True)) / MEMBERS
    apart = totals * (1.0 / CELLS) - average
    spread = (
        over_group(jnp.sum(squares + CELLS * (apart * apart), axis=0, keepdims=True))
        / MEMBERS
    )
    return average, 1.0 / jnp.sqrt(spread + 1e-05)


def stats_kernel(features, out):
    own_stats(features[...].reshape(CELLS, C).astype(F32), out)


def stats_call(features):
    return pl.pallas_call(
        stats_kernel,
        out_shape=jax.ShapeDtypeStruct((SLABS, 2, C), F32),
        in_specs=[VMEM],
        out_specs=VMEM,
        compiler_params=params(4),
        cost_estimate=cost(4, 1),
        name="stats",
    )(features)


def prep_kernel(
    features,
    step,
    codes,
    guides,
    table,
    time_weight,
    film,
    conv_two,
    head,
    mod,
    mix,
    base,
    roots,
):
    time_value = jnp.broadcast_to(step[...].astype(F32).reshape(1, 1), (1, C))
    roots[...] = sampler_roots(time_value)
    mod[0:1, :] = modulate(time_value, codes, table, time_weight, film)
    share = own_weight(guides[...].astype(F32))
    mix[...] = compose(conv_two, head[...], share)
    base[...] = direct(features, head[...], share)


def prep_call(*operands):
    return pl.pallas_call(
        prep_kernel,
        out_shape=(
            jax.ShapeDtypeStruct((8, 2 * C), F32),
            jax.ShapeDtypeStruct((9 * ROWS, 4 * C), F32),
            jax.ShapeDtypeStruct((ROWS, HW), F32),
            jax.ShapeDtypeStruct((4, C), F32),
        ),
        in_specs=[VMEM] * len(operands),
        out_specs=(VMEM,) * 4,
        compiler_params=params(60),
        cost_estimate=cost(1, 4),
        name="prep",
    )(*operands)


def exact(left, right):
    parts = three_parts(left)
    coarse = right.astype(BF16)
    fine = (right - coarse.astype(F32)).astype(BF16)
    product = jnp.dot(parts, coarse, preferred_element_type=F32) + jnp.dot(
        parts, fine, preferred_element_type=F32
    )
    return three_sum(product)


def plan(step_value):
    frac = (step_value / 1000.0 + 0.008) / 1.008
    return jnp.cos(frac * (math.pi / 2.0)) ** 2


def sampler_roots(time_value):
    now_bar = plan(time_value)
    next_bar = plan(time_value - STRIDE)
    return jnp.sqrt(
        jnp.concatenate([1.0 - now_bar, now_bar, next_bar, 1.0 - next_bar], axis=0)
    )


def modulate(time_value, codes, table, time_weight, film):
    lane = lax.broadcasted_iota(jnp.int32, (1, EMB // 2), 1)
    angles = time_value * jnp.exp(
        -math.log(10000.0) * lane.astype(F32) / (EMB // 2)
    )
    sinus = jnp.concatenate([jnp.cos(angles), jnp.sin(angles)], axis=1)
    wanted = jnp.zeros((1, SLOTS * CODES), jnp.int32)
    for slot in range(SLOTS):
        wanted = jnp.where(lane // CODES == slot, codes[0:1, slot : slot + 1], wanted)
    one_hot = (lane % CODES == wanted).astype(F32)
    rows = jnp.broadcast_to(jnp.concatenate([sinus, one_hot], axis=1), (8, EMB + SLOTS * CODES))
    tables = jnp.concatenate([time_weight[...], table[...]], axis=0)
    embedding = silu(exact(rows, tables))
    return exact(embedding, film[...])[:1]


def own_weight(guides):
    term = lax.axis_index("cond")
    lane = lax.broadcasted_iota(jnp.int32, (1, TERMS), 1)
    values = guides
    others = jnp.sum(jnp.where(lane == 0, 0.0, values), axis=1, keepdims=True)
    mine = jnp.sum(jnp.where(lane == term, values, 0.0), axis=1, keepdims=True)
    return jnp.where(term == 0, TERMS - others, mine) * (1.0 / 16.0)


def three_sum(product):
    return product[:ROWS] + (product[ROWS : 2 * ROWS] + product[2 * ROWS : 3 * ROWS])


def compose(conv_two, head, weight):
    head_rows = jnp.concatenate([head, head], axis=0)
    upper = lax.broadcasted_iota(jnp.int32, (ROWS, C), 0) < LAT
    composed = three_sum(dot_last(three_parts(head_rows), conv_two[...])) * weight
    nothing = jnp.zeros((ROWS, C), F32)
    rows = []
    for near in range(9):
        blocks = []
        for plane in range(DEP_DEV + 2):
            at = [
                composed[:, (tap * 9 + near) * C : (tap * 9 + near + 1) * C]
                if 0 <= tap < 3
                else nothing
                for tap in (plane, plane - 1)
            ]
            blocks.append(jnp.where(upper, at[0], at[1]))
        rows.append(jnp.concatenate(blocks, axis=1))
    return jnp.concatenate(rows, axis=0)


def direct(features, head, weight):
    head_rows = jnp.concatenate([head, head], axis=0)
    upper = lax.broadcasted_iota(jnp.int32, (ROWS, C), 0) < LAT
    wide = jnp.concatenate(
        [jnp.where(upper, head_rows, 0.0), jnp.where(upper, 0.0, head_rows)], axis=1
    )
    both = jnp.concatenate([features[0], features[1]], axis=1)
    return three_sum(dot_last(three_parts(wide), both)) * weight


def rim_planes(swapped):
    slab = lax.axis_index("slab")
    first = slab % 2 == 0
    low = jnp.where(first, swapped[1], swapped[0])
    high = jnp.where(first, swapped[0], swapped[1])
    return [jnp.where(slab > 0, low, 0.0), jnp.where(slab < SLABS - 1, high, 0.0)]


def store_planes(held, planes):
    held[0:W, :] = jnp.zeros((W, held.shape[1]), BF16)
    held[W + HW :, :] = jnp.zeros((W, held.shape[1]), BF16)
    for at, values in enumerate(planes):
        held[W : W + HW, at * C : (at + 1) * C] = values.astype(BF16)


def block(weight, tap, row, col):
    at = ((tap * 3 + row) * 3 + col) * C
    return weight[at : at + C, :]


def shifted_sum(part, side):
    column = lax.broadcasted_iota(jnp.int32, (HW, C), 0) % W
    side[8 : 8 + HW, :] = part[0]
    before = jnp.where(column == 0, 0.0, side[7 : 7 + HW, :])
    side[8 : 8 + HW, :] = part[2]
    after = jnp.where(column == W - 1, 0.0, side[9 : 9 + HW, :])
    return part[1] + before + after


def conv_kernel(every, odd, even, own, weight, mod, out, out_stats, held, norm, side):
    del mod
    average, scale = all_stats(every)
    shift = -average * scale
    norm[0:1, :] = scale
    norm[1:2, :] = shift

    def act(values):
        return silu(values.astype(F32) * scale + shift)

    parity = lax.axis_index("slab") % 2
    low, high = rim_planes([act(even[parity]), act(odd[1 - parity])])
    store_planes(held, [low, act(own[0]), act(own[1]), high])
    zero = jnp.zeros((C, C), BF16)
    products = []
    for col in range(3):
        product = None
        for row in range(3):
            right = jnp.concatenate(
                [
                    jnp.concatenate(
                        [
                            zero if tap is None else block(weight, tap, row, col)
                            for tap in taps
                        ],
                        axis=1,
                    )
                    for taps in [(0, None), (1, 0), (2, 1), (None, 2)]
                ],
                axis=0,
            )
            term = jnp.dot(
                held[row * W : row * W + HW, :], right, preferred_element_type=F32
            )
            product = term if product is None else product + term
        products.append(product)
    for plane in range(DEP_DEV):
        out[plane] = shifted_sum(
            [product[:, plane * C : (plane + 1) * C] for product in products], side
        )
    own_stats(out[...].reshape(CELLS, C), out_stats)


def conv_call(*operands):
    return pl.pallas_call(
        conv_kernel,
        out_shape=(
            jax.ShapeDtypeStruct((DEP_DEV, HW, C), F32),
            jax.ShapeDtypeStruct((SLABS, 2, C), F32),
            jax.ShapeDtypeStruct((HW + 2 * W, 4 * C), BF16),
            jax.ShapeDtypeStruct((8, C), F32),
        ),
        in_specs=[VMEM] * len(operands),
        out_specs=(VMEM,) * 4,
        scratch_shapes=[pltpu.VMEM((HW + 16, C), F32)],
        compiler_params=params(16),
        cost_estimate=cost(2, 32),
        name="conv",
    )(*operands)


def far_planes(norm, even, odd, near, weight, held, side):
    def act(values):
        return silu(values.astype(F32) * norm[0:1, :] + norm[1:2, :])

    parity = lax.axis_index("slab") % 2
    store_planes(held, rim_planes([act(even[1 - parity]), act(odd[parity])]))
    planes = []
    for plane in range(2):
        left = []
        for row in range(3):
            rows = pl.ds(row * W, HW)
            if plane == 0:
                left += [held[rows, :C], near[rows, : 2 * C]]
            else:
                left += [near[rows, 2 * C :], held[rows, C:]]
        left = jnp.concatenate(left, axis=1)

        def right(col):
            return jnp.concatenate(
                [block(weight, tap, row, col) for row in range(3) for tap in range(3)], axis=0
            )

        pair = jnp.concatenate([right(0), right(1)], axis=1)
        wide = jnp.dot(left, pair, preferred_element_type=F32)
        narrow = jnp.dot(left, right(2), preferred_element_type=F32)
        planes.append(shifted_sum([wide[:, :C], wide[:, C:], narrow], side))
    return planes


def mixed(planes, weights, held):
    for at, values in enumerate(planes):
        held[:, at * C : (at + 1) * C] = values.astype(BF16)
    coarse = weights.astype(BF16).astype(F32)
    pair = jnp.concatenate([coarse, weights - coarse], axis=0).astype(BF16)
    product = dot_last(pair, held[...])
    return product[: 9 * ROWS] + product[9 * ROWS :]


def head_kernel(
    every,
    first,
    norm,
    odd,
    even,
    near,
    weight,
    mod,
    mix,
    base,
    out,
    rim,
    side,
    held,
):
    far = far_planes(norm, even, odd, near, weight, rim, side)
    average, scale = all_stats(every)
    factor = scale * (1.0 + mod[0:1, :C])
    shift = mod[0:1, C:] - average * factor

    def act(values):
        return silu(values * factor + shift)

    slab = lax.axis_index("slab")
    low = jnp.where(slab > 0, act(far[0]), 0.0)
    high = jnp.where(slab < SLABS - 1, act(far[1]), 0.0)
    product = mixed([low, act(first[0]), act(first[1]), high], mix[...], held)
    at = lax.broadcasted_iota(jnp.int32, (ROWS, HW), 1)
    summed = base[...]
    for col in range(3):
        part = [product[(row * 3 + col) * ROWS : (row * 3 + col + 1) * ROWS] for row in range(3)]
        values = (
            part[1]
            + jnp.where(at < W, 0.0, pltpu.roll(part[0], W, 1))
            + jnp.where(at >= HW - W, 0.0, pltpu.roll(part[2], HW - W, 1))
        )
        if col == 0:
            values = jnp.where(at % W == 0, 0.0, pltpu.roll(values, 1, 1))
        if col == 2:
            values = jnp.where(at % W == W - 1, 0.0, pltpu.roll(values, HW - 1, 1))
        summed = summed + values
    for target in range(TERMS):
        piece = summed[:, target * SHARE : (target + 1) * SHARE]
        out[target] = jnp.concatenate([piece[:LAT], piece[LAT:]], axis=1)


def head_call(*operands):
    return pl.pallas_call(
        head_kernel,
        out_shape=jax.ShapeDtypeStruct((TERMS, LAT, DEP_DEV * SHARE), F32),
        in_specs=[VMEM] * len(operands),
        out_specs=VMEM,
        scratch_shapes=[
            pltpu.VMEM((HW + 2 * W, 2 * C), BF16),
            pltpu.VMEM((HW + 16, C), F32),
            pltpu.VMEM((HW, 4 * C), BF16),
        ],
        compiler_params=params(20),
        cost_estimate=cost(1, 32),
        name="head",
    )(*operands)


def final_kernel(roots, pieces, latent, guided, stepped):
    total = jnp.sum(pieces[...], axis=0)
    noise_now, root_now, root_next, noise_next = [roots[at : at + 1, :SHARE] for at in range(4)]
    for plane in range(DEP_DEV):
        value = total[:, plane * SHARE : (plane + 1) * SHARE]
        clean = (latent[:, plane, :] - noise_now * value) / root_now
        guided[:, plane, :] = value
        stepped[:, plane, :] = root_next * clean + noise_next * value


def final_call(roots, pieces, latent):
    shape = jax.ShapeDtypeStruct((LAT, DEP_DEV, SHARE), F32)
    return pl.pallas_call(
        final_kernel,
        out_shape=(shape, shape),
        in_specs=[VMEM, VMEM, VMEM],
        out_specs=(VMEM, VMEM),
        compiler_params=params(2),
        name="final",
    )(roots, pieces, latent)


EVEN_PAIRS = [(at, at ^ 1) for at in range(SLABS)]
ODD_PAIRS = [(at, ((at + 1) ^ 1) - 1) for at in range(1, SLABS - 1)]


def per_device(
    features,
    latent,
    cond_codes,
    guide_codes,
    timestep,
    code_table,
    time_weight,
    film_weight,
    conv_one,
    conv_two,
    head_weight,
):
    planes = features.reshape(DEP_DEV, HW, C)
    even = lax.ppermute(planes, "slab", EVEN_PAIRS)
    odd = lax.ppermute(planes, "slab", ODD_PAIRS)
    stats = stats_call(planes)
    mod, mix, base, roots = prep_call(
        planes,
        timestep,
        cond_codes,
        guide_codes.reshape(1, TERMS),
        code_table.reshape(SLOTS * CODES, EMB),
        time_weight,
        film_weight,
        conv_two.reshape(TAPS * C, C),
        head_weight.T,
    )
    every = lax.all_to_all(stats, "slab", 0, 0)
    weight = conv_one.reshape(TAPS * C, C)
    first, stats, near, norm = conv_call(every, odd, even, planes, weight, mod)
    every = lax.all_to_all(stats, "slab", 0, 0)
    pieces = head_call(every, first, norm, odd, even, near, weight, mod, mix, base)
    pieces = lax.all_to_all(pieces, "cond", 0, 0)
    return final_call(roots, pieces, latent)


def solution(mesh):
    placed = (
        P("cond", "slab", None, None, None),
        P(None, "slab", "cond"),
        P("cond", None),
        P(),
        P(),
        P(),
        P(),
        P(),
        P(),
        P(),
        P(),
    )
    return jax.shard_map(
        per_device,
        mesh=mesh,
        in_specs=placed,
        out_specs=(P(None, "slab", "cond"), P(None, "slab", "cond")),
        check_vma=False,
    )
```

```python
import math

import jax
import jax.numpy as jnp
from jax import lax
from jax.experimental import pallas as pl
from jax.experimental.pallas import tpu as pltpu
from jax.sharding import PartitionSpec as P

C = 128
GROUPS = 32
PER_GROUP = C // GROUPS
EMB = 256
LAT = 4
SLOTS = 8
CODES = 16
STRIDE = 20
DEP_DEV = 2
H = 16
W = 64
HW = H * W
TERMS = 16
SHARE = HW // TERMS
SLABS = 16
CELLS = DEP_DEV * HW
MEMBERS = float(SLABS * CELLS * PER_GROUP)
TAPS = 27
F32 = jnp.float32
BF16 = jnp.bfloat16
ROWS = 2 * LAT

VMEM = pl.BlockSpec(memory_space=pltpu.VMEM)


def params(mebibytes):
    return pltpu.CompilerParams(vmem_limit_bytes=mebibytes * 1024 * 1024)


def cost(gigaflops, mebibytes):
    return pl.CostEstimate(
        flops=gigaflops * 10**9, bytes_accessed=mebibytes * 2**20, transcendentals=0
    )


def dot_last(left, right):
    return lax.dot_general(left, right, (((1,), (1,)), ((), ())), preferred_element_type=F32)


def silu(values):
    half = 0.5 * values
    return half + half * jnp.tanh(half)


def column_sum(values):
    partial = jnp.sum(values.reshape(-1, W, C), axis=0)
    return jnp.sum(partial, axis=0, keepdims=True)


def own_stats(values, out_ref):
    pivot = jnp.sum(values[:W], axis=0, keepdims=True) * (1.0 / W)
    apart = values - pivot
    total = column_sum(apart)
    square = column_sum(apart * apart) - total * total * (1.0 / CELLS)
    both = jnp.concatenate([total + CELLS * pivot, square], axis=0)
    out_ref[...] = jnp.broadcast_to(both[None], (SLABS, 2, C))


def over_group(values):
    lane = lax.broadcasted_iota(jnp.int32, values.shape, 1)
    for step in (1, 2):
        other = jnp.where(
            lane // step % 2 == 0, pltpu.roll(values, C - step, 1), pltpu.roll(values, step, 1)
        )
        values = values + other
    return values


def three_parts(values):
    high = values.astype(BF16).astype(F32)
    rest = values - high
    middle = rest.astype(BF16).astype(F32)
    low = rest - middle
    zero = jnp.zeros_like(values)
    return jnp.concatenate([high, middle, low, zero], axis=0).astype(BF16)


def all_stats(every_ref):
    every = every_ref[...]
    totals = every[:, 0, :]
    squares = every[:, 1, :]
    average = over_group(jnp.sum(totals, axis=0, keepdims=True)) / MEMBERS
    apart = totals * (1.0 / CELLS) - average
    spread = (
        over_group(jnp.sum(squares + CELLS * (apart * apart), axis=0, keepdims=True))
        / MEMBERS
    )
    return average, 1.0 / jnp.sqrt(spread + 1e-05)


def stats_kernel(features, out):
    own_stats(features[...].reshape(CELLS, C).astype(F32), out)


def stats_call(features):
    return pl.pallas_call(
        stats_kernel,
        out_shape=jax.ShapeDtypeStruct((SLABS, 2, C), F32),
        in_specs=[VMEM],
        out_specs=VMEM,
        compiler_params=params(4),
        cost_estimate=cost(4, 1),
        name="stats",
    )(features)


def prep_kernel(
    features,
    step,
    codes,
    guides,
    table,
    time_weight,
    film,
    conv_two,
    head,
    mod,
    mix,
    base,
    roots,
):
    time_value = jnp.broadcast_to(step[...].astype(F32).reshape(1, 1), (1, C))
    roots[...] = sampler_roots(time_value)
    mod[0:1, :] = modulate(time_value, codes, table, time_weight, film)
    share = own_weight(guides[...].astype(F32))
    mix[...] = compose(conv_two, head[...], share)
    base[...] = direct(features, head[...], share)


def prep_call(*operands):
    return pl.pallas_call(
        prep_kernel,
        out_shape=(
            jax.ShapeDtypeStruct((8, 2 * C), F32),
            jax.ShapeDtypeStruct((9 * ROWS, 4 * C), F32),
            jax.ShapeDtypeStruct((ROWS, HW), F32),
            jax.ShapeDtypeStruct((4, C), F32),
        ),
        in_specs=[VMEM] * len(operands),
        out_specs=(VMEM,) * 4,
        compiler_params=params(60),
        cost_estimate=cost(1, 4),
        name="prep",
    )(*operands)


def carry_kernel(mod, out):
    out[...] = mod[...]


def carry_call(mod):
    return pl.pallas_call(
        carry_kernel,
        out_shape=jax.ShapeDtypeStruct(mod.shape, F32),
        in_specs=[VMEM],
        out_specs=VMEM,
        compiler_params=params(2),
        cost_estimate=cost(1, 1),
        name="carry",
    )(mod)


def exact(left, right):
    parts = three_parts(left)
    coarse = right.astype(BF16)
    fine = (right - coarse.astype(F32)).astype(BF16)
    product = jnp.dot(parts, coarse, preferred_element_type=F32) + jnp.dot(
        parts, fine, preferred_element_type=F32
    )
    return three_sum(product)


def plan(step_value):
    frac = (step_value / 1000.0 + 0.008) / 1.008
    return jnp.cos(frac * (math.pi / 2.0)) ** 2


def sampler_roots(time_value):
    now_bar = plan(time_value)
    next_bar = plan(time_value - STRIDE)
    return jnp.sqrt(
        jnp.concatenate([1.0 - now_bar, now_bar, next_bar, 1.0 - next_bar], axis=0)
    )


def modulate(time_value, codes, table, time_weight, film):
    lane = lax.broadcasted_iota(jnp.int32, (1, EMB // 2), 1)
    angles = time_value * jnp.exp(
        -math.log(10000.0) * lane.astype(F32) / (EMB // 2)
    )
    sinus = jnp.concatenate([jnp.cos(angles), jnp.sin(angles)], axis=1)
    wanted = jnp.zeros((1, SLOTS * CODES), jnp.int32)
    for slot in range(SLOTS):
        wanted = jnp.where(lane // CODES == slot, codes[0:1, slot : slot + 1], wanted)
    one_hot = (lane % CODES == wanted).astype(F32)
    rows = jnp.broadcast_to(jnp.concatenate([sinus, one_hot], axis=1), (8, EMB + SLOTS * CODES))
    tables = jnp.concatenate([time_weight[...], table[...]], axis=0)
    embedding = silu(exact(rows, tables))
    return exact(embedding, film[...])[:1]


def own_weight(guides):
    term = lax.axis_index("cond")
    lane = lax.broadcasted_iota(jnp.int32, (1, TERMS), 1)
    values = guides
    others = jnp.sum(jnp.where(lane == 0, 0.0, values), axis=1, keepdims=True)
    mine = jnp.sum(jnp.where(lane == term, values, 0.0), axis=1, keepdims=True)
    return jnp.where(term == 0, TERMS - others, mine) * (1.0 / 16.0)


def three_sum(product):
    return product[:ROWS] + (product[ROWS : 2 * ROWS] + product[2 * ROWS : 3 * ROWS])


def compose(conv_two, head, weight):
    head_rows = jnp.concatenate([head, head], axis=0)
    upper = lax.broadcasted_iota(jnp.int32, (ROWS, C), 0) < LAT
    composed = three_sum(dot_last(three_parts(head_rows), conv_two[...])) * weight
    nothing = jnp.zeros((ROWS, C), F32)
    rows = []
    for near in range(9):
        blocks = []
        for plane in range(DEP_DEV + 2):
            at = [
                composed[:, (tap * 9 + near) * C : (tap * 9 + near + 1) * C]
                if 0 <= tap < 3
                else nothing
                for tap in (plane, plane - 1)
            ]
            blocks.append(jnp.where(upper, at[0], at[1]))
        rows.append(jnp.concatenate(blocks, axis=1))
    return jnp.concatenate(rows, axis=0)


def direct(features, head, weight):
    head_rows = jnp.concatenate([head, head], axis=0)
    upper = lax.broadcasted_iota(jnp.int32, (ROWS, C), 0) < LAT
    wide = jnp.concatenate(
        [jnp.where(upper, head_rows, 0.0), jnp.where(upper, 0.0, head_rows)], axis=1
    )
    both = jnp.concatenate([features[0], features[1]], axis=1)
    return three_sum(dot_last(three_parts(wide), both)) * weight


def rim_planes(swapped):
    slab = lax.axis_index("slab")
    first = slab % 2 == 0
    low = jnp.where(first, swapped[1], swapped[0])
    high = jnp.where(first, swapped[0], swapped[1])
    return [jnp.where(slab > 0, low, 0.0), jnp.where(slab < SLABS - 1, high, 0.0)]


def store_planes(held, planes):
    held[0:W, :] = jnp.zeros((W, held.shape[1]), BF16)
    held[W + HW :, :] = jnp.zeros((W, held.shape[1]), BF16)
    for at, values in enumerate(planes):
        held[W : W + HW, at * C : (at + 1) * C] = values.astype(BF16)


def block(weight, tap, row, col):
    at = ((tap * 3 + row) * 3 + col) * C
    return weight[at : at + C, :]


def shifted_sum(part, side):
    column = lax.broadcasted_iota(jnp.int32, (HW, C), 0) % W
    side[8 : 8 + HW, :] = part[0]
    before = jnp.where(column == 0, 0.0, side[7 : 7 + HW, :])
    side[8 : 8 + HW, :] = part[2]
    after = jnp.where(column == W - 1, 0.0, side[9 : 9 + HW, :])
    return part[1] + before + after


def conv_kernel(every, odd, even, own, weight, mod, out, out_stats, held, norm, side):
    del mod
    average, scale = all_stats(every)
    shift = -average * scale
    norm[0:1, :] = scale
    norm[1:2, :] = shift

    def act(values):
        return silu(values.astype(F32) * scale + shift)

    parity = lax.axis_index("slab") % 2
    low, high = rim_planes([act(even[parity]), act(odd[1 - parity])])
    store_planes(held, [low, act(own[0]), act(own[1]), high])
    zero = jnp.zeros((C, C), BF16)
    products = []
    for col in range(3):
        product = None
        for row in range(3):
            right = jnp.concatenate(
                [
                    jnp.concatenate(
                        [
                            zero if tap is None else block(weight, tap, row, col)
                            for tap in taps
                        ],
                        axis=1,
                    )
                    for taps in [(0, None), (1, 0), (2, 1), (None, 2)]
                ],
                axis=0,
            )
            term = jnp.dot(
                held[row * W : row * W + HW, :], right, preferred_element_type=F32
            )
            product = term if product is None else product + term
        products.append(product)
    for plane in range(DEP_DEV):
        out[plane] = shifted_sum(
            [product[:, plane * C : (plane + 1) * C] for product in products], side
        )
    own_stats(out[...].reshape(CELLS, C), out_stats)


def conv_call(*operands):
    return pl.pallas_call(
        conv_kernel,
        out_shape=(
            jax.ShapeDtypeStruct((DEP_DEV, HW, C), F32),
            jax.ShapeDtypeStruct((SLABS, 2, C), F32),
            jax.ShapeDtypeStruct((HW + 2 * W, 4 * C), BF16),
            jax.ShapeDtypeStruct((8, C), F32),
        ),
        in_specs=[VMEM] * len(operands),
        out_specs=(VMEM,) * 4,
        scratch_shapes=[pltpu.VMEM((HW + 16, C), F32)],
        compiler_params=params(16),
        cost_estimate=cost(2, 32),
        name="conv",
    )(*operands)


def far_planes(norm, even, odd, near, weight, held, side):
    def act(values):
        return silu(values.astype(F32) * norm[0:1, :] + norm[1:2, :])

    parity = lax.axis_index("slab") % 2
    store_planes(held, rim_planes([act(even[1 - parity]), act(odd[parity])]))
    planes = []
    for plane in range(2):
        left = []
        for row in range(3):
            rows = pl.ds(row * W, HW)
            if plane == 0:
                left += [held[rows, :C], near[rows, : 2 * C]]
            else:
                left += [near[rows, 2 * C :], held[rows, C:]]
        left = jnp.concatenate(left, axis=1)

        def right(col):
            return jnp.concatenate(
                [block(weight, tap, row, col) for row in range(3) for tap in range(3)], axis=0
            )

        pair = jnp.concatenate([right(0), right(1)], axis=1)
        wide = jnp.dot(left, pair, preferred_element_type=F32)
        narrow = jnp.dot(left, right(2), preferred_element_type=F32)
        planes.append(shifted_sum([wide[:, :C], wide[:, C:], narrow], side))
    return planes


def mixed(planes, weights, held):
    for at, values in enumerate(planes):
        held[:, at * C : (at + 1) * C] = values.astype(BF16)
    coarse = weights.astype(BF16).astype(F32)
    pair = jnp.concatenate([coarse, weights - coarse], axis=0).astype(BF16)
    product = dot_last(pair, held[...])
    return product[: 9 * ROWS] + product[9 * ROWS :]


def head_kernel(
    every,
    first,
    norm,
    odd,
    even,
    near,
    weight,
    mod,
    mix,
    base,
    out,
    rim,
    side,
    held,
):
    far = far_planes(norm, even, odd, near, weight, rim, side)
    average, scale = all_stats(every)
    factor = scale * (1.0 + mod[0:1, :C])
    shift = mod[0:1, C:] - average * factor

    def act(values):
        return silu(values * factor + shift)

    slab = lax.axis_index("slab")
    low = jnp.where(slab > 0, act(far[0]), 0.0)
    high = jnp.where(slab < SLABS - 1, act(far[1]), 0.0)
    product = mixed([low, act(first[0]), act(first[1]), high], mix[...], held)
    at = lax.broadcasted_iota(jnp.int32, (ROWS, HW), 1)
    summed = base[...]
    for col in range(3):
        part = [product[(row * 3 + col) * ROWS : (row * 3 + col + 1) * ROWS] for row in range(3)]
        values = (
            part[1]
            + jnp.where(at < W, 0.0, pltpu.roll(part[0], W, 1))
            + jnp.where(at >= HW - W, 0.0, pltpu.roll(part[2], HW - W, 1))
        )
        if col == 0:
            values = jnp.where(at % W == 0, 0.0, pltpu.roll(values, 1, 1))
        if col == 2:
            values = jnp.where(at % W == W - 1, 0.0, pltpu.roll(values, HW - 1, 1))
        summed = summed + values
    for target in range(TERMS):
        piece = summed[:, target * SHARE : (target + 1) * SHARE]
        out[target] = jnp.concatenate([piece[:LAT], piece[LAT:]], axis=1)


def head_call(*operands):
    return pl.pallas_call(
        head_kernel,
        out_shape=jax.ShapeDtypeStruct((TERMS, LAT, DEP_DEV * SHARE), F32),
        in_specs=[VMEM] * len(operands),
        out_specs=VMEM,
        scratch_shapes=[
            pltpu.VMEM((HW + 2 * W, 2 * C), BF16),
            pltpu.VMEM((HW + 16, C), F32),
            pltpu.VMEM((HW, 4 * C), BF16),
        ],
        compiler_params=params(20),
        cost_estimate=cost(1, 32),
        name="head",
    )(*operands)


def final_kernel(roots, pieces, latent, guided, stepped):
    total = jnp.sum(pieces[...], axis=0)
    noise_now, root_now, root_next, noise_next = [roots[at : at + 1, :SHARE] for at in range(4)]
    for plane in range(DEP_DEV):
        value = total[:, plane * SHARE : (plane + 1) * SHARE]
        clean = (latent[:, plane, :] - noise_now * value) / root_now
        guided[:, plane, :] = value
        stepped[:, plane, :] = root_next * clean + noise_next * value


def final_call(roots, pieces, latent):
    shape = jax.ShapeDtypeStruct((LAT, DEP_DEV, SHARE), F32)
    return pl.pallas_call(
        final_kernel,
        out_shape=(shape, shape),
        in_specs=[VMEM, VMEM, VMEM],
        out_specs=(VMEM, VMEM),
        compiler_params=params(2),
        name="final",
    )(roots, pieces, latent)


EVEN_PAIRS = [(at, at ^ 1) for at in range(SLABS)]
ODD_PAIRS = [(at, ((at + 1) ^ 1) - 1) for at in range(1, SLABS - 1)]


def per_device(
    features,
    latent,
    cond_codes,
    guide_codes,
    timestep,
    code_table,
    time_weight,
    film_weight,
    conv_one,
    conv_two,
    head_weight,
):
    planes = features.reshape(DEP_DEV, HW, C)
    even = lax.ppermute(planes, "slab", EVEN_PAIRS)
    odd = lax.ppermute(planes, "slab", ODD_PAIRS)
    stats = stats_call(planes)
    mod, mix, base, roots = prep_call(
        planes,
        timestep,
        cond_codes,
        guide_codes.reshape(1, TERMS),
        code_table.reshape(SLOTS * CODES, EMB),
        time_weight,
        film_weight,
        conv_two.reshape(TAPS * C, C),
        head_weight.T,
    )
    every = lax.all_to_all(stats, "slab", 0, 0)
    weight = conv_one.reshape(TAPS * C, C)
    mod = carry_call(mod)
    first, stats, near, norm = conv_call(every, odd, even, planes, weight, mod)
    every = lax.all_to_all(stats, "slab", 0, 0)
    pieces = head_call(every, first, norm, odd, even, near, weight, mod, mix, base)
    pieces = lax.all_to_all(pieces, "cond", 0, 0)
    return final_call(roots, pieces, latent)


def solution(mesh):
    placed = (
        P("cond", "slab", None, None, None),
        P(None, "slab", "cond"),
        P("cond", None),
        P(),
        P(),
        P(),
        P(),
        P(),
        P(),
        P(),
        P(),
    )
    return jax.shard_map(
        per_device,
        mesh=mesh,
        in_specs=placed,
        out_specs=(P(None, "slab", "cond"), P(None, "slab", "cond")),
        check_vma=False,
    )
```
